512 devices in a mesh: img: 32 (over x_hi, y, core), txt: 16 (over z, x_lo).
Axes of the slice: x: 4 (x_hi: 2, x_lo: 2; x = x_hi * 2 + x_lo), y: 8, z: 8, core: 2. Of those that a mesh axis runs over, the one named last changes fastest.
Arguments:
- image_student: bfloat16 [24576, 512], P(('img', 'txt')), may hold values from -16 to 16
- text_student: bfloat16 [24576, 512], P(('img', 'txt')), may hold values from -16 to 16
- image_teacher: bfloat16 [24576, 768], P(('img', 'txt')), may hold values from -16 to 16
- text_teacher: bfloat16 [24576, 768], P(('img', 'txt')), may hold values from -16 to 16
Outputs:
- image_loss: float32 [24576], P(('img', 'txt'))
- text_loss: float32 [24576], P(('img', 'txt'))
- mean_loss: float32 [], replicated
The draws below stay inside these ranges and needn't reach their ends.
All inputs are finite; a program needn't handle non-finite values.
Results may differ from the reference program's by a relative error of at most 0.0003.
Values may be sent and summed in bfloat16 or wider, within the bound.
No kernel may reach another device: no remote copies, remote signals or barrier semaphores. Data moves between devices by JAX's collectives and lax.ppermute only.
A program may use at most 64 MiB of HBM per device.

```python
import math
import jax
import jax.numpy as jnp
from jax import lax

DS = 512
DT = 768
TOKENS = 24576


def finish_draw(values):
    return jnp.clip(values, -16.0, 16.0).astype(jnp.bfloat16)


def draw_image_student(key, part):
    key = jax.random.fold_in(key, 1)
    values = jax.random.normal(key, (TOKENS, DS), jnp.float32)
    return finish_draw(values)


def draw_text_student(key, part):
    key = jax.random.fold_in(key, 2)
    values = jax.random.normal(key, (TOKENS, DS), jnp.float32)
    return finish_draw(values)


def draw_image_teacher(key, part):
    key = jax.random.fold_in(key, 3)
    values = jax.random.normal(key, (TOKENS, DT), jnp.float32)
    return finish_draw(values)


def draw_text_teacher(key, part):
    key = jax.random.fold_in(key, 4)
    values = jax.random.normal(key, (TOKENS, DT), jnp.float32)
    return finish_draw(values)


def setup_inputs(seed: int = 0) -> dict:
    arg_keys = jax.random.split(jax.random.key(seed), 5)
    image_student = draw_image_student(jax.random.fold_in(arg_keys[4], 71), 0)
    text_student = draw_text_student(jax.random.fold_in(arg_keys[4], 71), 0)
    image_teacher = draw_image_teacher(jax.random.fold_in(arg_keys[4], 71), 0)
    text_teacher = draw_text_teacher(jax.random.fold_in(arg_keys[4], 71), 0)
    return dict(image_student=image_student, text_student=text_student, image_teacher=image_teacher, text_teacher=text_teacher)


mixing = 0.5

def losses(own_student, other_student, own_teacher):
    count = own_student.shape[0]
    block = math.gcd(count, 512)
    own_s = own_student.astype(jnp.float32)
    other_s = other_student.astype(jnp.float32)
    own_t = own_teacher.astype(jnp.float32)
    sfactor = 2.0 / math.sqrt(own_s.shape[1])
    tfactor = 3.0 / math.sqrt(own_t.shape[1])
    columns = jnp.arange(count, dtype=jnp.int32)

    def one_block(start):
        rows_s = lax.dynamic_slice_in_dim(own_s, start, block, 0)
        rows_t = lax.dynamic_slice_in_dim(own_t, start, block, 0)
        logits = jnp.dot(rows_s, other_s.T, precision=lax.Precision.HIGHEST) * sfactor
        gram = jnp.dot(rows_t, own_t.T, precision=lax.Precision.HIGHEST) * tfactor
        rows = start + jnp.arange(block, dtype=jnp.int32)
        same = rows[:, None] == columns[None, :]
        spread = jax.nn.logsumexp(logits, axis=1)
        target = jax.nn.softmax(jnp.where(same, -jnp.inf, gram), axis=1)
        soft = lax.optimization_barrier(jnp.sum(target * logits, axis=1))
        diagonal = lax.optimization_barrier(jnp.sum(jnp.where(same, logits, 0.0), axis=1))
        return spread - (1.0 - mixing) * diagonal - mixing * soft
    starts = (jnp.arange(count // block) * block).astype(jnp.int32)
    return lax.map(one_block, starts).reshape(count)

def reference(image_student, text_student, image_teacher, text_teacher):
    image_loss = losses(image_student, text_student, image_teacher)
    text_loss = losses(text_student, image_student, text_teacher)
    mean_loss = (jnp.sum(image_loss) + jnp.sum(text_loss)) / (2.0 * TOKENS)
    return (image_loss, text_loss, mean_loss)
```

```python
import functools
import math

import jax
import jax.numpy as jnp
from jax import lax
from jax.experimental import pallas as pl
from jax.experimental.pallas import tpu as pltpu
from jax.sharding import PartitionSpec as P

AXES = ("img", "txt")
LOG2E = 1.0 / math.log(2.0)
LOW = -1e30
SHARD = 48
BLOCK = 64
CHUNK = 256


def place(x, y, z, c):
    return (((x // 2) * 8 + y) * 2 + c) * 16 + z * 2 + x % 2


def everywhere():
    return [
        (x, y, z, c) for x in range(4) for y in range(8) for z in range(8) for c in range(2)
    ]


CORE_PAIRS = [(place(x, y, z, c), place(x, y, z, 1 - c)) for x, y, z, c in everywhere()]
X_PAIRS = [
    (place(x, y, z, c), place(x ^ 1 if c == 0 else 3 - x, y, z, c)) for x, y, z, c in everywhere()
]
LINES = [[place(x, y, z, 0) for z in range(8)] for x in range(4) for y in range(8)] + [
    [place(x, y, z, 1) for y in range(8)] for x in range(4) for z in range(8)
]
ROW_GROUPS = [
    [place(x, y, z, c) for z in range(8) for x in pair]
    for pair in ((0, 1), (3, 2))
    for y in range(8)
    for c in range(2)
]
COLUMN_GROUPS = [
    [place(x, y, z, c) for y in range(8) for x in pair for c in range(2)]
    for pair in ((0, 3), (1, 2))
    for z in range(8)
]


def dot(left, right):
    return lax.dot_general(
        left, right, (((1,), (1,)), ((), ())), preferred_element_type=jnp.float32
    )


def tile_kernel(ds, dt, own, other, row_out, col_out, a, b, l, g, h, ml, mg, colbuf, rowbuf, asem, bsem):
    rows, cols = a.shape[0], b.shape[0]
    chunks = cols // CHUNK
    blocks = rows // BLOCK
    img = lax.axis_index("img")
    txt = lax.axis_index("txt")
    core = img % 2
    y = (img // 2) % 8
    x_hi = img // 16
    x_lo = txt % 2
    z = txt // 2
    kl = 2.0 / math.sqrt(ds) * LOG2E
    kt = 3.0 / math.sqrt(dt) * LOG2E

    def copies(row_src, col_src, c):
        out = []
        for k in range(rows // SHARD):
            out.append(
                pltpu.make_async_copy(
                    row_src.at[k, c], a.at[pl.ds(k * SHARD, SHARD)], asem.at[k]
                )
            )
        for j in range(chunks):
            out.append(
                pltpu.make_async_copy(
                    col_src.at[pl.ds(j * CHUNK, CHUNK)], b.at[pl.ds(j * CHUNK, CHUNK)], bsem.at[j]
                )
            )
        return out

    flat_own = own.reshape(cols, own.shape[-1])
    flat_other = other.reshape(cols, own.shape[-1])

    @pl.when(core == 0)
    def _():
        for copy in copies(own, flat_other, 0):
            copy.start()

    @pl.when(core == 1)
    def _():
        for copy in copies(other, flat_own, 1):
            copy.start()

    ml[...] = jnp.full(ml.shape, LOW, jnp.float32)
    mg[...] = jnp.full(mg.shape, LOW, jnp.float32)
    waits = copies(own, flat_other, 0)
    for copy in waits[: rows // SHARD]:
        copy.wait()
    r0 = pl.multiple_of(z * (2 * SHARD), 2 * SHARD)
    c0 = y * (4 * SHARD) + (1 - core) * SHARD

    for j in range(chunks):
        waits[rows // SHARD + j].wait()
        span = pl.ds(j * CHUNK, CHUNK)
        l[j] = dot(a[:, :ds], b[span, :ds])
        g[j] = dot(a[:, ds : ds + dt], b[span, ds + dt :])
        h[...] = dot(a[:, ds + dt :], b[span, ds : ds + dt])

        @pl.when((c0 < (j + 1) * CHUNK) & (c0 + SHARD > j * CHUNK))
        def _():
            here = pl.ds(r0, SHARD)
            r = lax.broadcasted_iota(jnp.int32, (SHARD, CHUNK), 0)
            s = lax.broadcasted_iota(jnp.int32, (SHARD, CHUNK), 1) + (j * CHUNK - c0)
            same = r == s
            g[j, here, :] = jnp.where(same, LOW, g[j, here, :])
            h[here, :] = jnp.where(same, LOW, h[here, :])

        def peaks(i, so_far):
            cl, ch = so_far
            here = pl.ds(pl.multiple_of(i * BLOCK, BLOCK), BLOCK)
            lv = l[j, here, :]
            gv = g[j, here, :]
            hv = h[here, :]
            ml[here, :] = jnp.maximum(ml[here, :], jnp.maximum(lv[:, :128], lv[:, 128:]))
            mg[here, :] = jnp.maximum(mg[here, :], jnp.maximum(gv[:, :128], gv[:, 128:]))
            cl = jnp.maximum(cl, jnp.max(lv.reshape(BLOCK // 8, 8, CHUNK), axis=0))
            ch = jnp.maximum(ch, jnp.max(hv.reshape(BLOCK // 8, 8, CHUNK), axis=0))
            return cl, ch

        low = jnp.full((8, CHUNK), LOW, jnp.float32)
        cl, ch = lax.fori_loop(0, blocks, peaks, (low, low))
        cl = jnp.max(cl, axis=0, keepdims=True)
        ch = jnp.max(ch, axis=0, keepdims=True)

        def sums(i, so_far):
            total, mass, weighted = so_far
            here = pl.ds(pl.multiple_of(i * BLOCK, BLOCK), BLOCK)
            lv = l[j, here, :]
            el = jnp.exp2((lv - cl) * kl)
            eh = jnp.exp2((h[here, :] - ch) * kt)
            wh = eh * lv
            fold = lambda v: jnp.sum(v.reshape(BLOCK // 8, 8, CHUNK), axis=0)
            return total + fold(el), mass + fold(eh), weighted + fold(wh)

        zero = jnp.zeros((8, CHUNK), jnp.float32)
        total, mass, weighted = lax.fori_loop(0, blocks, sums, (zero, zero, zero))
        total = jnp.sum(total, axis=0, keepdims=True)
        mass = jnp.sum(mass, axis=0, keepdims=True)
        weighted = jnp.sum(weighted, axis=0, keepdims=True)
        colbuf[0:1, span] = cl * (kl / LOG2E) + jnp.log(total)
        colbuf[1:2, span] = ch * (kt / LOG2E) + jnp.log(mass)
        colbuf[2:3, span] = weighted / mass * (kl / LOG2E)

    lane = lax.broadcasted_iota(jnp.int32, (BLOCK, 128), 1)

    def along(i, _):
        here = pl.ds(pl.multiple_of(i * BLOCK, BLOCK), BLOCK)
        pl_ = jnp.max(ml[here, :], axis=1, keepdims=True)
        pg = jnp.max(mg[here, :], axis=1, keepdims=True)
        total = jnp.zeros((BLOCK, 128), jnp.float32)
        mass = jnp.zeros((BLOCK, 128), jnp.float32)
        weighted = jnp.zeros((BLOCK, 128), jnp.float32)
        for j in range(chunks):
            for q in range(CHUNK // 128):
                lanes = pl.ds(q * 128, 128)
                lv = l[j, here, lanes]
                total += jnp.exp2((lv - pl_) * kl)
                eg = jnp.exp2((g[j, here, lanes] - pg) * kt)
                mass += eg
                weighted += eg * lv
        total = jnp.sum(total, axis=1, keepdims=True)
        mass = jnp.sum(mass, axis=1, keepdims=True)
        weighted = jnp.sum(weighted, axis=1, keepdims=True)
        one = pl_ * (kl / LOG2E) + jnp.log(total)
        two = pg * (kt / LOG2E) + jnp.log(mass)
        three = weighted / mass * (kl / LOG2E)
        rowbuf[here, :] = jnp.where(lane == 0, one, jnp.where(lane == 1, two, three))
        return 0

    lax.fori_loop(0, blocks, along, 0)

    xi_row = x_lo ^ x_hi
    xi_col = x_hi
    for k in range(rows // SHARD):
        piece = rowbuf[k * SHARD : (k + 1) * SHARD, :]
        turned = jnp.swapaxes(piece, 0, 1)[:8, :]
        row_out[(k // 2) * 2 + (xi_row ^ (k % 2))] = turned
    for k in range(cols // SHARD):
        rel, other_core = (k // 2) % 2, k % 2
        col_out[(k // 4) * 4 + 2 * (xi_col ^ rel) + (1 - other_core)] = colbuf[
            :, k * SHARD : (k + 1) * SHARD
        ]


def tile(own, other, ds, dt):
    width = own.shape[-1]
    rows, cols = 16 * SHARD, 32 * SHARD
    chunks = cols // CHUNK
    return pl.pallas_call(
        functools.partial(tile_kernel, ds, dt),
        out_shape=(
            jax.ShapeDtypeStruct((rows // SHARD, 8, SHARD), jnp.float32),
            jax.ShapeDtypeStruct((cols // SHARD, 8, SHARD), jnp.float32),
        ),
        in_specs=[pl.BlockSpec(memory_space=pl.ANY)] * 2,
        out_specs=[pl.BlockSpec(memory_space=pltpu.VMEM)] * 2,
        scratch_shapes=[
            pltpu.VMEM((rows, width), jnp.bfloat16),
            pltpu.VMEM((cols, width), jnp.bfloat16),
            pltpu.VMEM((chunks, rows, CHUNK), jnp.float32),
            pltpu.VMEM((chunks, rows, CHUNK), jnp.float32),
            pltpu.VMEM((rows, CHUNK), jnp.float32),
            pltpu.VMEM((rows, 128), jnp.float32),
            pltpu.VMEM((rows, 128), jnp.float32),
            pltpu.VMEM((8, cols), jnp.float32),
            pltpu.VMEM((rows, 128), jnp.float32),
            pltpu.SemaphoreType.DMA((rows // SHARD,)),
            pltpu.SemaphoreType.DMA((chunks,)),
        ],
        compiler_params=pltpu.CompilerParams(vmem_limit_bytes=40 * 1024 * 1024),
        cost_estimate=pl.CostEstimate(
            flops=2 * rows * cols * width, bytes_accessed=2 * (rows + cols) * width, transcendentals=4 * rows * cols
        ),
    )(own, other)


def joined(parts):
    lse, mark, mean = parts[:, 0], parts[:, 1], parts[:, 2]
    peak = jnp.max(lse, axis=0)
    spread = peak + jnp.log(jnp.sum(jnp.exp(lse - peak), axis=0))
    weight = jnp.exp(mark - jnp.max(mark, axis=0))
    return spread, jnp.sum(weight * mean, axis=0) / jnp.sum(weight, axis=0)


def shared_sum(value, groups):
    count = len(groups[0])
    sent = jnp.full((count, 1, 128), value)
    return jnp.sum(lax.all_to_all(sent, AXES, 0, 0, axis_index_groups=groups)[:, 0, 0])


def shards(image_student, text_student, image_teacher, text_teacher):
    ds, dt = image_student.shape[1], image_teacher.shape[1]
    core = lax.axis_index("img") % 2
    image_side = jnp.concatenate([image_student, image_teacher, text_teacher], axis=1)
    text_side = jnp.concatenate([text_student, text_teacher, image_teacher], axis=1)
    mine = jnp.where(core == 0, image_side, text_side)
    theirs = jnp.where(core == 0, text_side, image_side)
    chip = jnp.concatenate([mine, lax.ppermute(theirs, AXES, CORE_PAIRS)], axis=0)
    pair = jnp.concatenate([chip, lax.ppermute(chip, AXES, X_PAIRS)], axis=0)
    line = lax.all_gather(pair, AXES, axis=0, tiled=True, axis_index_groups=LINES)
    other = lax.ppermute(line, AXES, CORE_PAIRS)
    shape = (16, 2, SHARD, line.shape[1])
    row_stats, col_stats = tile(line.reshape(shape), other.reshape(shape), ds, dt)
    row_parts = lax.all_to_all(row_stats, AXES, 0, 0, axis_index_groups=ROW_GROUPS)
    col_parts = lax.all_to_all(col_stats, AXES, 0, 0, axis_index_groups=COLUMN_GROUPS)
    diagonal = jnp.sum(
        image_student.astype(jnp.float32) * text_student.astype(jnp.float32), axis=1
    ) * (2.0 / math.sqrt(ds))
    image_spread, image_soft = joined(row_parts)
    text_spread, text_soft = joined(col_parts)
    image_loss = image_spread - 0.5 * diagonal - 0.5 * image_soft
    text_loss = text_spread - 0.5 * diagonal - 0.5 * text_soft
    overall = jnp.sum(image_loss) + jnp.sum(text_loss)
    overall = shared_sum(shared_sum(overall, COLUMN_GROUPS), ROW_GROUPS)
    return image_loss, text_loss, overall / (2.0 * SHARD * 512)


def solution(mesh):
    spec = P(("img", "txt"), None)
    return jax.shard_map(
        shards,
        mesh=mesh,
        in_specs=(spec, spec, spec, spec),
        out_specs=(P(("img", "txt")), P(("img", "txt")), P()),
        check_vma=False,
    )
```

```python
import functools
import math

import jax
import jax.numpy as jnp
from jax import lax
from jax.experimental import pallas as pl
from jax.experimental.pallas import tpu as pltpu
from jax.sharding import PartitionSpec as P

AXES = ("img", "txt")
LOG2E = 1.0 / math.log(2.0)
LOW = -1e30
SHARD = 48
CHUNK = 256
BLOCK = 128


def place(x, y, z, c):
    return (((x // 2) * 8 + y) * 2 + c) * 16 + z * 2 + x % 2


def everywhere():
    return [
        (x, y, z, c) for x in range(4) for y in range(8) for z in range(8) for c in range(2)
    ]


ROW_X = ((0, 1), (3, 2))
COL_X = ((0, 3), (1, 2))
CORE_PAIRS = [(place(x, y, z, c), place(x, y, z, 1 - c)) for x, y, z, c in everywhere()]
X_PAIRS = [
    (place(x, y, z, c), place(x ^ 1 if c == 0 else 3 - x, y, z, c)) for x, y, z, c in everywhere()
]
UP, DOWN = (
    [
        (place(x, y, z, c), place(x, y, (z + s) % 8, c) if c == 0 else place(x, (y + s) % 8, z, c))
        for x, y, z, c in everywhere()
    ]
    for s in (1, -1)
)
STAT_GROUPS = [[place(x, y, z, 0) for z in range(8) for x in pair] for pair in ROW_X for y in range(8)] + [
    [place(x, y, z, 1) for y in range(8) for x in pair] for pair in COL_X for z in range(8)
]
SUM_GROUPS = [
    [place(pair[e], y, k, 0) for y in range(8) for pair in ROW_X]
    + [place(pair[e], k, z, 1) for z in range(8) for pair in COL_X]
    for k in range(8)
    for e in range(2)
]


def where_am_i():
    img = lax.axis_index("img")
    txt = lax.axis_index("txt")
    x_hi, x_lo = img // 16, txt % 2
    core = img % 2
    return jnp.where(core == 0, txt // 2, (img // 2) % 8), jnp.where(core == 0, x_hi ^ x_lo, x_hi)


def dot(left, right):
    return lax.dot_general(
        left, right, (((1,), (1,)), ((), ())), preferred_element_type=jnp.float32
    )


def pack_kernel(image_s, text_s, image_t, text_t, mine, theirs):
    ds, dt = image_s.shape[1], image_t.shape[1]
    core = lax.axis_index("img") % 2

    def fill(out, student, first, second):
        out[:, :ds] = student[...]
        out[:, ds : ds + dt] = first[...]
        out[:, ds + dt :] = second[...]

    @pl.when(core == 0)
    def _():
        fill(mine, image_s, image_t, text_t)
        fill(theirs, text_s, text_t, image_t)

    @pl.when(core == 1)
    def _():
        fill(mine, text_s, text_t, image_t)
        fill(theirs, image_s, image_t, text_t)


def pack(image_s, text_s, image_t, text_t):
    shape = jax.ShapeDtypeStruct((SHARD, image_s.shape[1] + 2 * image_t.shape[1]), jnp.bfloat16)
    vmem = pl.BlockSpec(memory_space=pltpu.VMEM)
    return pl.pallas_call(
        pack_kernel,
        out_shape=(shape, shape),
        in_specs=[vmem] * 4,
        out_specs=[vmem] * 2,
        compiler_params=pltpu.CompilerParams(vmem_limit_bytes=4 * 1024 * 1024),
    )(image_s, text_s, image_t, text_t)


def tile_kernel(ds, dt, units, *refs):
    own, other = refs[:units], refs[units : 2 * units]
    out, l, g, stats = refs[2 * units :]
    rows = 32 * SHARD
    chunks = rows // CHUNK
    line, xi = where_am_i()
    kl = 2.0 / math.sqrt(ds) * LOG2E
    kt = 3.0 / math.sqrt(dt) * LOG2E

    def piece(refs, start, stop, low, high):
        parts, at = [], 0
        for ref in refs:
            size = ref.shape[0]
            a, b = max(start - at, 0), min(stop - at, size)
            if a < b:
                parts.append(ref[a:b, low:high])
            at += size
        return jnp.concatenate(parts, axis=0) if len(parts) > 1 else parts[0]

    def products(j):
        n = j % 2
        a, b = j * CHUNK, (j + 1) * CHUNK
        l[n] = dot(piece(other, 0, rows, 0, ds), piece(own, a, b, 0, ds))
        g[n] = dot(piece(other, 0, rows, ds + dt, ds + 2 * dt), piece(own, a, b, ds, ds + dt))

    def summary(j):
        n = j % 2
        diagonal = jnp.zeros((1, CHUNK), jnp.float32)
        if j == 0:
            s = lax.broadcasted_iota(jnp.int32, (2 * SHARD, CHUNK), 0)
            r = lax.broadcasted_iota(jnp.int32, (2 * SHARD, CHUNK), 1)
            same = (r < 2 * SHARD) & (s == jnp.where(r < SHARD, r + SHARD, r - SHARD))
            g[n, : 2 * SHARD, :] = jnp.where(same, LOW, g[n, : 2 * SHARD, :])
            diagonal = jnp.sum(jnp.where(same, l[n, : 2 * SHARD, :], 0.0), axis=0, keepdims=True)
        blocks = [slice(i, i + BLOCK) for i in range(0, rows, BLOCK)]

        def eights(v):
            return v.reshape(BLOCK // 8, 8, CHUNK)

        pl_ = pg = jnp.full((8, CHUNK), LOW, jnp.float32)
        for here in blocks:
            pl_ = jnp.maximum(pl_, jnp.max(eights(l[n, here, :]), axis=0))
            pg = jnp.maximum(pg, jnp.max(eights(g[n, here, :]), axis=0))
        pl_ = jnp.max(pl_, axis=0, keepdims=True)
        pg = jnp.max(pg, axis=0, keepdims=True)
        total = mass = weighted = jnp.zeros((8, CHUNK), jnp.float32)
        for here in blocks:
            lv = l[n, here, :]
            e = jnp.exp2((g[n, here, :] - pg) * kt)
            total += jnp.sum(eights(jnp.exp2((lv - pl_) * kl)), axis=0)
            mass += jnp.sum(eights(e), axis=0)
            weighted += jnp.sum(eights(e * lv), axis=0)
        total = jnp.sum(total, axis=0, keepdims=True)
        mass = jnp.sum(mass, axis=0, keepdims=True)
        weighted = jnp.sum(weighted, axis=0, keepdims=True)
        to = slice(j * CHUNK, (j + 1) * CHUNK)
        stats[0:1, to] = pl_ * (kl / LOG2E) + jnp.log(total)
        stats[1:2, to] = pg * (kt / LOG2E) + jnp.log(mass)
        stats[2:3, to] = weighted / mass * (kl / LOG2E)
        stats[3:4, to] = diagonal * (kl / LOG2E)

    products(0)
    for j in range(1, chunks):
        products(j)
        summary(j - 1)
    summary(chunks - 1)

    for k, step in enumerate((0, 7, 1, 6, 2, 5, 3, 4)):
        v = stats[:4, k * 4 * SHARD : (k + 1) * 4 * SHARD]
        v = jnp.where(xi == 0, v, jnp.concatenate([v[:, 2 * SHARD :], v[:, : 2 * SHARD]], axis=1))
        row = pl.ds(lax.rem(line + step, 8), 1)
        for n in range(4):
            out[0, n, row, :] = v[n : n + 1, :128]
            out[0, 4 + n // 2, row, (n % 2) * 64 : (n % 2 + 1) * 64] = v[n : n + 1, 128:]
    for k in range(1, out.shape[0]):
        out[k] = out[0]


def tile(own, other, ds, dt):
    rows = 32 * SHARD
    vmem = pl.BlockSpec(memory_space=pltpu.VMEM)
    return pl.pallas_call(
        functools.partial(tile_kernel, ds, dt, len(own)),
        out_shape=jax.ShapeDtypeStruct((16, 6, 8, 128), jnp.float32),
        in_specs=[vmem] * (len(own) + len(other)),
        out_specs=vmem,
        scratch_shapes=[
            pltpu.VMEM((2, rows, CHUNK), jnp.float32),
            pltpu.VMEM((2, rows, CHUNK), jnp.float32),
            pltpu.VMEM((8, rows), jnp.float32),
        ],
        compiler_params=pltpu.CompilerParams(vmem_limit_bytes=24 * 1024 * 1024),
        cost_estimate=pl.CostEstimate(
            flops=2 * rows * rows * (ds + dt), bytes_accessed=8 * rows * (ds + dt), transcendentals=2 * rows * rows
        ),
    )(*own, *other)


def finish_kernel(parts, mine, total, held):
    line, xi = where_am_i()
    count = parts.shape[0]

    def losses(lse, mark, mean, diagonal):
        top, high = lse(0), mark(0)
        for k in range(1, count):
            top = jnp.maximum(top, lse(k))
            high = jnp.maximum(high, mark(k))
        spread = mass = weighted = own = jnp.zeros_like(top)
        for k in range(count):
            e = jnp.exp(mark(k) - high)
            spread += jnp.exp(lse(k) - top)
            mass += e
            weighted += e * mean(k)
            own += diagonal(k)
        return top + jnp.log(spread) - 0.5 * own - 0.5 * weighted / mass

    one = losses(*(lambda k, n=n: parts[k, n] for n in range(4)))
    two = losses(*(lambda k, n=n: parts[k, 4 + n // 2][:, (n % 2) * 64 : (n % 2 + 1) * 64] for n in range(4)))
    held[:, :128] = one
    held[:, 128:] = jnp.concatenate([two, two], axis=1)
    v = held[pl.ds(line, 1), :]
    mine[...] = jnp.where(xi == 0, v[:, :128], v[:, 2 * SHARD : 2 * SHARD + 128])
    total[...] = jnp.full(total.shape, jnp.sum(one) + jnp.sum(two), jnp.float32)


def finish(parts):
    vmem = pl.BlockSpec(memory_space=pltpu.VMEM)
    return pl.pallas_call(
        finish_kernel,
        out_shape=(
            jax.ShapeDtypeStruct((1, 128), jnp.float32),
            jax.ShapeDtypeStruct((32, 1, 128), jnp.float32),
        ),
        in_specs=[vmem],
        out_specs=[vmem] * 2,
        scratch_shapes=[pltpu.VMEM((8, 256), jnp.float32)],
        compiler_params=pltpu.CompilerParams(vmem_limit_bytes=4 * 1024 * 1024),
    )(parts)


def shards(image_student, text_student, image_teacher, text_teacher):
    ds, dt = image_student.shape[1], image_teacher.shape[1]
    core = lax.axis_index("img") % 2

    def swap(v):
        return lax.ppermute(v, AXES, CORE_PAIRS)

    mine, theirs = pack(image_student, text_student, image_teacher, text_teacher)
    chip = jnp.concatenate([mine, swap(theirs)], axis=0)
    pair = jnp.concatenate([chip, lax.ppermute(chip, AXES, X_PAIRS)], axis=0)
    own, other = [pair], [swap(pair)]
    up = down = pair
    for _ in range(3):
        up, down = lax.ppermute(up, AXES, UP), lax.ppermute(down, AXES, DOWN)
        own += [up, down]
        other += [swap(up), swap(down)]
    half = pair.shape[0] // 2
    up, down = lax.ppermute(up[:half], AXES, UP), lax.ppermute(down[half:], AXES, DOWN)
    own += [up, down]
    other += [swap(up), swap(down)]
    stats = tile(own, other, ds, dt)
    parts = lax.all_to_all(stats, AXES, 0, 0, axis_index_groups=STAT_GROUPS)
    losses, total = finish(parts)
    first, second = losses[0, :SHARD], swap(losses)[0, SHARD : 2 * SHARD]
    image_loss = jnp.where(core == 0, first, second)
    text_loss = jnp.where(core == 0, second, first)
    totals = lax.all_to_all(total, AXES, 0, 0, axis_index_groups=SUM_GROUPS)
    return image_loss, text_loss, jnp.sum(totals[:, 0, 0]) / (2.0 * SHARD * 512)


def solution(mesh):
    spec = P(("img", "txt"), None)
    return jax.shard_map(
        shards,
        mesh=mesh,
        in_specs=(spec, spec, spec, spec),
        out_specs=(P(("img", "txt")), P(("img", "txt")), P()),
        check_vma=False,
    )
```

```python
import functools
import math

import jax
import jax.numpy as jnp
from jax import lax
from jax.experimental import pallas as pl
from jax.experimental.pallas import tpu as pltpu
from jax.sharding import PartitionSpec as P

AXES = ("img", "txt")
LOG2E = 1.0 / math.log(2.0)
LOW = -1e30
SHARD = 48
CHUNK = 256
BLOCK = 128


def place(x, y, z, c):
    return (((x // 2) * 8 + y) * 2 + c) * 16 + z * 2 + x % 2


def everywhere():
    return [
        (x, y, z, c) for x in range(4) for y in range(8) for z in range(8) for c in range(2)
    ]


ROW_X = ((0, 1), (3, 2))
COL_X = ((0, 3), (1, 2))
CORE_PAIRS = [(place(x, y, z, c), place(x, y, z, 1 - c)) for x, y, z, c in everywhere()]
X_PAIRS = [
    (place(x, y, z, c), place(x ^ 1 if c == 0 else 3 - x, y, z, c)) for x, y, z, c in everywhere()
]
X_CROSS = [
    (place(x, y, z, c), place(x ^ 1 if c == 1 else 3 - x, y, z, 1 - c)) for x, y, z, c in everywhere()
]
UP, DOWN = (
    [
        (place(x, y, z, c), place(x, y, (z + s) % 8, c) if c == 0 else place(x, (y + s) % 8, z, c))
        for x, y, z, c in everywhere()
    ]
    for s in (1, -1)
)
STAT_GROUPS = [[place(x, y, z, 0) for z in range(8) for x in pair] for pair in ROW_X for y in range(8)] + [
    [place(x, y, z, 1) for y in range(8) for x in pair] for pair in COL_X for z in range(8)
]
SUM_GROUPS = [
    [place(pair[e], y, k, 0) for y in range(8) for pair in ROW_X]
    + [place(pair[e], k, z, 1) for z in range(8) for pair in COL_X]
    for k in range(8)
    for e in range(2)
]


def where_am_i():
    img = lax.axis_index("img")
    txt = lax.axis_index("txt")
    x_hi, x_lo = img // 16, txt % 2
    core = img % 2
    return jnp.where(core == 0, txt // 2, (img // 2) % 8), jnp.where(core == 0, x_hi ^ x_lo, x_hi)


def dot(left, right):
    return lax.dot_general(
        left, right, (((1,), (1,)), ((), ())), preferred_element_type=jnp.float32
    )


def pack_kernel(image_s, text_s, image_t, text_t, mine, theirs, sems):
    ds, dt = image_s.shape[1], image_t.shape[1]
    core = lax.axis_index("img") % 2

    def copies(image_out, text_out):
        parts = (pl.ds(0, ds), pl.ds(ds, dt), pl.ds(ds + dt, dt))
        out = []
        for n, source in enumerate((image_s, image_t, text_t)):
            out.append(pltpu.make_async_copy(source, image_out.at[:, parts[n]], sems.at[n]))
        for n, source in enumerate((text_s, text_t, image_t)):
            out.append(pltpu.make_async_copy(source, text_out.at[:, parts[n]], sems.at[3 + n]))
        return out

    @pl.when(core == 0)
    def _():
        for copy in copies(mine, theirs):
            copy.start()

    @pl.when(core == 1)
    def _():
        for copy in copies(theirs, mine):
            copy.start()

    for copy in copies(mine, theirs):
        copy.wait()


def pack(image_s, text_s, image_t, text_t):
    shape = jax.ShapeDtypeStruct((SHARD, image_s.shape[1] + 2 * image_t.shape[1]), jnp.bfloat16)
    return pl.pallas_call(
        pack_kernel,
        out_shape=(shape, shape),
        in_specs=[pl.BlockSpec(memory_space=pl.ANY)] * 4,
        out_specs=[pl.BlockSpec(memory_space=pltpu.VMEM)] * 2,
        scratch_shapes=[pltpu.SemaphoreType.DMA((6,))],
        compiler_params=pltpu.CompilerParams(vmem_limit_bytes=60 * 1024 * 1024),
    )(image_s, text_s, image_t, text_t)


def piece(refs, start, stop, low, high):
    parts, at = [], 0
    for ref in refs:
        size = ref.shape[0]
        a, b = max(start - at, 0), min(stop - at, size)
        if a < b:
            parts.append(ref[a:b, low:high])
        at += size
    return jnp.concatenate(parts, axis=0) if len(parts) > 1 else parts[0]


def products(ds, dt, own, other, lanes, rows, l, g):
    l[: rows[1] - rows[0], :] = dot(piece(other, *rows, 0, ds), piece(own, *lanes, 0, ds))
    g[: rows[1] - rows[0], :] = dot(piece(other, *rows, ds + dt, ds + 2 * dt), piece(own, *lanes, ds, ds + dt))


def summary(ds, dt, l, g, rows, first):
    kl = 2.0 / math.sqrt(ds) * LOG2E
    kt = 3.0 / math.sqrt(dt) * LOG2E
    diagonal = jnp.zeros((1, CHUNK), jnp.float32)
    if first:
        s = lax.broadcasted_iota(jnp.int32, (2 * SHARD, CHUNK), 0)
        r = lax.broadcasted_iota(jnp.int32, (2 * SHARD, CHUNK), 1)
        same = (r < 2 * SHARD) & (s == jnp.where(r < SHARD, r + SHARD, r - SHARD))
        g[: 2 * SHARD, :] = jnp.where(same, LOW, g[: 2 * SHARD, :])
        diagonal = jnp.sum(jnp.where(same, l[: 2 * SHARD, :], 0.0), axis=0, keepdims=True)
    blocks = [slice(i, min(i + BLOCK, rows)) for i in range(0, rows, BLOCK)]

    def eights(v):
        return v.reshape(v.shape[0] // 8, 8, CHUNK)

    top = high = jnp.full((8, CHUNK), LOW, jnp.float32)
    for here in blocks:
        top = jnp.maximum(top, jnp.max(eights(l[here, :]), axis=0))
        high = jnp.maximum(high, jnp.max(eights(g[here, :]), axis=0))
    top = jnp.max(top, axis=0, keepdims=True)
    high = jnp.max(high, axis=0, keepdims=True)
    total = mass = weighted = jnp.zeros((8, CHUNK), jnp.float32)
    for here in blocks:
        lv = l[here, :]
        e = jnp.exp2((g[here, :] - high) * kt)
        total += jnp.sum(eights(jnp.exp2((lv - top) * kl)), axis=0)
        mass += jnp.sum(eights(e), axis=0)
        weighted += jnp.sum(eights(e * lv), axis=0)
    total = jnp.sum(total, axis=0, keepdims=True)
    mass = jnp.sum(mass, axis=0, keepdims=True)
    weighted = jnp.sum(weighted, axis=0, keepdims=True)
    return (
        top * (kl / LOG2E) + jnp.log(total),
        high * (kt / LOG2E) + jnp.log(mass),
        weighted / mass * (kl / LOG2E),
        diagonal * (kl / LOG2E),
    )


def early_kernel(ds, dt, units, *refs):
    own, other = refs[:units], refs[units : 2 * units]
    out, l, g = refs[2 * units :]
    rows = units * 4 * SHARD
    chunks = rows // CHUNK

    def multiply(j):
        products(ds, dt, own, other, (j * CHUNK, (j + 1) * CHUNK), (0, rows), l.at[j % 2], g.at[j % 2])

    multiply(0)
    for j in range(chunks):
        if j + 1 < chunks:
            multiply(j + 1)
        for n, v in enumerate(summary(ds, dt, l.at[j % 2], g.at[j % 2], rows, j == 0)):
            out[n : n + 1, j * CHUNK : (j + 1) * CHUNK] = v


def early(own, other, ds, dt):
    rows = len(own) * 4 * SHARD
    chunks = rows // CHUNK
    vmem = pl.BlockSpec(memory_space=pltpu.VMEM)
    work = rows * chunks * CHUNK
    return pl.pallas_call(
        functools.partial(early_kernel, ds, dt, len(own)),
        out_shape=jax.ShapeDtypeStruct((8, chunks * CHUNK), jnp.float32),
        in_specs=[vmem] * (len(own) + len(other)),
        out_specs=vmem,
        scratch_shapes=[pltpu.VMEM((2, rows, CHUNK), jnp.float32)] * 2,
        compiler_params=pltpu.CompilerParams(vmem_limit_bytes=20 * 1024 * 1024),
        cost_estimate=pl.CostEstimate(
            flops=2 * work * (ds + dt), bytes_accessed=8 * rows * (ds + dt), transcendentals=2 * work
        ),
    )(*own, *other)


def late_kernel(ds, dt, units, known, *refs):
    own, other = refs[:units], refs[units : 2 * units]
    before, out, l, g, ls, gs, stats = refs[2 * units :]
    rows = units * 4 * SHARD
    chunks = rows // CHUNK
    done = known // CHUNK
    line, xi = where_am_i()

    def lanes(j):
        return j * CHUNK, (j + 1) * CHUNK

    for j in range(done):
        products(ds, dt, own, other, lanes(j), (known, rows), ls.at[j], gs.at[j])
    for j in range(done, chunks):
        products(ds, dt, own, other, lanes(j), (0, rows), l.at[j % 2], g.at[j % 2])
        if j == done:
            for i in range(done):
                to = slice(*lanes(i))
                lse, mark, mean, _ = summary(ds, dt, ls.at[i], gs.at[i], rows - known, False)
                old_lse, old_mark, old_mean = (before[n : n + 1, to] for n in range(3))
                top = jnp.maximum(lse, old_lse)
                stats[0:1, to] = top + jnp.log(jnp.exp(lse - top) + jnp.exp(old_lse - top))
                top = jnp.maximum(mark, old_mark)
                one, two = jnp.exp(mark - top), jnp.exp(old_mark - top)
                stats[1:2, to] = top + jnp.log(one + two)
                stats[2:3, to] = (one * mean + two * old_mean) / (one + two)
                stats[3:4, to] = before[3:4, to]
        else:
            for n, v in enumerate(summary(ds, dt, l.at[(j - 1) % 2], g.at[(j - 1) % 2], rows, False)):
                stats[n : n + 1, slice(*lanes(j - 1))] = v
    for n, v in enumerate(summary(ds, dt, l.at[(chunks - 1) % 2], g.at[(chunks - 1) % 2], rows, False)):
        stats[n : n + 1, slice(*lanes(chunks - 1))] = v

    for k, step in enumerate((0, 7, 1, 6, 2, 5, 3, 4)):
        v = stats[:4, k * 4 * SHARD : (k + 1) * 4 * SHARD]
        v = jnp.where(xi == 0, v, jnp.concatenate([v[:, 2 * SHARD :], v[:, : 2 * SHARD]], axis=1))
        row = pl.ds(lax.rem(line + step, 8), 1)
        for n in range(4):
            out[0, n, row, :] = v[n : n + 1, :128]
            out[0, 4 + n // 2, row, (n % 2) * 64 : (n % 2 + 1) * 64] = v[n : n + 1, 128:]
    for k in range(1, out.shape[0]):
        out[k] = out[0]


def late(own, other, before, known, ds, dt):
    rows = len(own) * 4 * SHARD
    chunks, done = rows // CHUNK, known // CHUNK
    vmem = pl.BlockSpec(memory_space=pltpu.VMEM)
    work = rows * rows - known * done * CHUNK
    return pl.pallas_call(
        functools.partial(late_kernel, ds, dt, len(own), known),
        out_shape=jax.ShapeDtypeStruct((16, 6, 8, 128), jnp.float32),
        in_specs=[vmem] * (len(own) + len(other) + 1),
        out_specs=vmem,
        scratch_shapes=[pltpu.VMEM((2, rows, CHUNK), jnp.float32)] * 2
        + [pltpu.VMEM((done, rows - known, CHUNK), jnp.float32)] * 2
        + [pltpu.VMEM((8, rows), jnp.float32)],
        compiler_params=pltpu.CompilerParams(vmem_limit_bytes=20 * 1024 * 1024),
        cost_estimate=pl.CostEstimate(
            flops=2 * work * (ds + dt), bytes_accessed=8 * rows * (ds + dt), transcendentals=2 * work
        ),
    )(*own, *other, before)


def losses(parts, count, lse, mark, mean, diagonal):
    top, high = lse(0), mark(0)
    for k in range(1, count):
        top = jnp.maximum(top, lse(k))
        high = jnp.maximum(high, mark(k))
    spread = mass = weighted = own = jnp.zeros_like(top)
    for k in range(count):
        e = jnp.exp(mark(k) - high)
        spread += jnp.exp(lse(k) - top)
        mass += e
        weighted += e * mean(k)
        own += diagonal(k)
    return top + jnp.log(spread) - 0.5 * own - 0.5 * weighted / mass


def halves(parts, rows):
    count = parts.shape[0]
    return (
        losses(parts, count, *(lambda k, n=n: parts[k, n, rows, :] for n in range(4))),
        losses(
            parts,
            count,
            *(lambda k, n=n: parts[k, 4 + n // 2, rows, (n % 2) * 64 : (n % 2 + 1) * 64] for n in range(4)),
        ),
    )


def finish_kernel(parts, mine, total, held):
    line, xi = where_am_i()
    one, two = halves(parts, slice(0, 8))
    held[:, :128] = one
    held[:, 128:] = jnp.concatenate([two, two], axis=1)
    v = held[pl.ds(line, 1), :]
    mine[...] = jnp.where(xi == 0, v[:, :128], v[:, 2 * SHARD : 2 * SHARD + 128])
    total[...] = jnp.full(total.shape, jnp.sum(one) + jnp.sum(two), jnp.float32)


def finish(parts):
    vmem = pl.BlockSpec(memory_space=pltpu.VMEM)
    return pl.pallas_call(
        finish_kernel,
        out_shape=(
            jax.ShapeDtypeStruct((1, 128), jnp.float32),
            jax.ShapeDtypeStruct((32, 1, 128), jnp.float32),
        ),
        in_specs=[vmem],
        out_specs=[vmem] * 2,
        scratch_shapes=[pltpu.VMEM((8, 256), jnp.float32)],
        compiler_params=pltpu.CompilerParams(vmem_limit_bytes=4 * 1024 * 1024),
    )(parts)


def shards(image_student, text_student, image_teacher, text_teacher):
    ds, dt = image_student.shape[1], image_teacher.shape[1]
    core = lax.axis_index("img") % 2

    def swap(v):
        return lax.ppermute(v, AXES, CORE_PAIRS)

    mine, theirs = pack(image_student, text_student, image_teacher, text_teacher)
    across = lax.ppermute(mine, AXES, X_PAIRS)
    beyond = lax.ppermute(theirs, AXES, X_CROSS)
    pair = jnp.concatenate([mine, swap(theirs), across, beyond], axis=0)
    own, other = [pair], []
    ready, sent, up, down = [pair], [], pair, pair
    for _ in range(3):
        up, sent = lax.optimization_barrier((up, sent))
        other += sent
        up, down = lax.ppermute(up, AXES, UP), lax.ppermute(down, AXES, DOWN)
        sent = [swap(v) for v in ready]
        ready = [up, down]
        own += ready
    up, sent = lax.optimization_barrier((up, sent))
    last = lax.ppermute(up, AXES, UP)
    other += sent
    before, last = lax.optimization_barrier((early(own[:5], other[:5], ds, dt), last))
    known = 5 * pair.shape[0]
    other += [swap(v) for v in ready + [last]]
    stats = late(own + [last], other, before, known, ds, dt)
    parts = lax.all_to_all(stats, AXES, 0, 0, axis_index_groups=STAT_GROUPS)
    chip, total = finish(parts)
    first, second = chip[0, :SHARD], swap(chip)[0, SHARD : 2 * SHARD]
    image_loss = jnp.where(core == 0, first, second)
    text_loss = jnp.where(core == 0, second, first)
    totals = lax.all_to_all(total, AXES, 0, 0, axis_index_groups=SUM_GROUPS)
    return image_loss, text_loss, jnp.sum(totals[:, 0, 0]) / (2.0 * SHARD * 512)


def solution(mesh):
    spec = P(("img", "txt"), None)
    return jax.shard_map(
        shards,
        mesh=mesh,
        in_specs=(spec, spec, spec, spec),
        out_specs=(P(("img", "txt")), P(("img", "txt")), P()),
        check_vma=False,
    )
```

```python
import functools
import math

import jax
import jax.numpy as jnp
from jax import lax
from jax.experimental import pallas as pl
from jax.experimental.pallas import tpu as pltpu
from jax.sharding import PartitionSpec as P

AXES = ("img", "txt")
LOG2E = 1.0 / math.log(2.0)
LOW = -1e30
SHARD = 48
CHUNK = 256
BLOCK = 128
ORDER = (((0, 7, 1), 0), ((0, 7, 1), 1), ((6, 2), 0), ((6, 2), 1), ((5, 3, 4), 0), ((5, 3, 4), 1))


def place(x, y, z, c):
    return (((x // 2) * 8 + y) * 2 + c) * 16 + z * 2 + x % 2


def everywhere():
    return [
        (x, y, z, c) for x in range(4) for y in range(8) for z in range(8) for c in range(2)
    ]


ROW_X = ((0, 1), (3, 2))
COL_X = ((0, 3), (1, 2))
CORE_PAIRS = [(place(x, y, z, c), place(x, y, z, 1 - c)) for x, y, z, c in everywhere()]
X_PAIRS = [
    (place(x, y, z, c), place(x ^ 1 if c == 0 else 3 - x, y, z, c)) for x, y, z, c in everywhere()
]
UP, DOWN = (
    [
        (place(x, y, z, c), place(x, y, (z + s) % 8, c) if c == 0 else place(x, (y + s) % 8, z, c))
        for x, y, z, c in everywhere()
    ]
    for s in (1, -1)
)
STAT_GROUPS = [[place(x, y, z, 0) for z in range(8) for x in pair] for pair in ROW_X for y in range(8)] + [
    [place(x, y, z, 1) for y in range(8) for x in pair] for pair in COL_X for z in range(8)
]
SUM_GROUPS = [
    [place(pair[e], y, k, 0) for y in range(8) for pair in ROW_X]
    + [place(pair[e], k, z, 1) for z in range(8) for pair in COL_X]
    for k in range(8)
    for e in range(2)
]


def where_am_i():
    img = lax.axis_index("img")
    txt = lax.axis_index("txt")
    x_hi, x_lo = img // 16, txt % 2
    core = img % 2
    return jnp.where(core == 0, txt // 2, (img // 2) % 8), jnp.where(core == 0, x_hi ^ x_lo, x_hi)


def dot(left, right):
    return lax.dot_general(
        left, right, (((1,), (1,)), ((), ())), preferred_element_type=jnp.float32
    )


def pack_kernel(image_s, text_s, image_t, text_t, mine, theirs, sems):
    ds, dt = image_s.shape[1], image_t.shape[1]
    core = lax.axis_index("img") % 2

    def copies(image_out, text_out):
        parts = (pl.ds(0, ds), pl.ds(ds, dt), pl.ds(ds + dt, dt))
        out = []
        for n, source in enumerate((image_s, image_t, text_t)):
            out.append(pltpu.make_async_copy(source, image_out.at[:, parts[n]], sems.at[n]))
        for n, source in enumerate((text_s, text_t, image_t)):
            out.append(pltpu.make_async_copy(source, text_out.at[:, parts[n]], sems.at[3 + n]))
        return out

    @pl.when(core == 0)
    def _():
        for copy in copies(mine, theirs):
            copy.start()

    @pl.when(core == 1)
    def _():
        for copy in copies(theirs, mine):
            copy.start()

    for copy in copies(mine, theirs):
        copy.wait()


def pack(image_s, text_s, image_t, text_t):
    shape = jax.ShapeDtypeStruct((SHARD, image_s.shape[1] + 2 * image_t.shape[1]), jnp.bfloat16)
    return pl.pallas_call(
        pack_kernel,
        out_shape=(shape, shape),
        in_specs=[pl.BlockSpec(memory_space=pl.ANY)] * 4,
        out_specs=[pl.BlockSpec(memory_space=pltpu.VMEM)] * 2,
        scratch_shapes=[pltpu.SemaphoreType.DMA((6,))],
        compiler_params=pltpu.CompilerParams(vmem_limit_bytes=60 * 1024 * 1024),
    )(image_s, text_s, image_t, text_t)


def total_rows(refs):
    return sum(ref.shape[0] for ref in refs)


def piece(refs, start, stop, low, high):
    parts, at = [], 0
    for ref in refs:
        size = ref.shape[0]
        a, b = max(start - at, 0), min(stop - at, size)
        if a < b:
            parts.append(ref[a:b, low:high])
        at += size
    return jnp.concatenate(parts, axis=0) if len(parts) > 1 else parts[0]


def products(ds, dt, own, other, lanes, rows, l, g):
    l[: rows[1] - rows[0], :] = dot(piece(other, *rows, 0, ds), piece(own, *lanes, 0, ds))
    g[: rows[1] - rows[0], :] = dot(piece(other, *rows, ds + dt, ds + 2 * dt), piece(own, *lanes, ds, ds + dt))


def summary(ds, dt, l, g, rows, first):
    kl = 2.0 / math.sqrt(ds) * LOG2E
    kt = 3.0 / math.sqrt(dt) * LOG2E
    diagonal = jnp.zeros((1, CHUNK), jnp.float32)
    if first:
        s = lax.broadcasted_iota(jnp.int32, (2 * SHARD, CHUNK), 0)
        r = lax.broadcasted_iota(jnp.int32, (2 * SHARD, CHUNK), 1)
        same = (r < 2 * SHARD) & (s == jnp.where(r < SHARD, r + SHARD, r - SHARD))
        g[: 2 * SHARD, :] = jnp.where(same, LOW, g[: 2 * SHARD, :])
        diagonal = jnp.sum(jnp.where(same, l[: 2 * SHARD, :], 0.0), axis=0, keepdims=True)
    blocks = [slice(i, min(i + BLOCK, rows)) for i in range(0, rows, BLOCK)]

    def eights(v):
        return v.reshape(v.shape[0] // 8, 8, CHUNK)

    top = high = jnp.full((8, CHUNK), LOW, jnp.float32)
    for here in blocks:
        top = jnp.maximum(top, jnp.max(eights(l[here, :]), axis=0))
        high = jnp.maximum(high, jnp.max(eights(g[here, :]), axis=0))
    top = jnp.max(top, axis=0, keepdims=True)
    high = jnp.max(high, axis=0, keepdims=True)
    total = mass = weighted = jnp.zeros((8, CHUNK), jnp.float32)
    for here in blocks:
        lv = l[here, :]
        e = jnp.exp2((g[here, :] - high) * kt)
        total += jnp.sum(eights(jnp.exp2((lv - top) * kl)), axis=0)
        mass += jnp.sum(eights(e), axis=0)
        weighted += jnp.sum(eights(e * lv), axis=0)
    total = jnp.sum(total, axis=0, keepdims=True)
    mass = jnp.sum(mass, axis=0, keepdims=True)
    weighted = jnp.sum(weighted, axis=0, keepdims=True)
    return (
        top * (kl / LOG2E) + jnp.log(total),
        high * (kt / LOG2E) + jnp.log(mass),
        weighted / mass * (kl / LOG2E),
        diagonal * (kl / LOG2E),
    )


def early_kernel(ds, dt, units, *refs):
    own, other = refs[:units], refs[units : 2 * units]
    out, l, g = refs[2 * units :]
    rows = total_rows(own)
    chunks = rows // CHUNK

    def multiply(j):
        products(ds, dt, own, other, (j * CHUNK, (j + 1) * CHUNK), (0, rows), l.at[j % 2], g.at[j % 2])

    multiply(0)
    for j in range(chunks):
        if j + 1 < chunks:
            multiply(j + 1)
        for n, v in enumerate(summary(ds, dt, l.at[j % 2], g.at[j % 2], rows, j == 0)):
            out[n : n + 1, j * CHUNK : (j + 1) * CHUNK] = v


def early(own, other, ds, dt):
    rows = total_rows(own)
    chunks = rows // CHUNK
    vmem = pl.BlockSpec(memory_space=pltpu.VMEM)
    work = rows * chunks * CHUNK
    return pl.pallas_call(
        functools.partial(early_kernel, ds, dt, len(own)),
        out_shape=jax.ShapeDtypeStruct((8, chunks * CHUNK), jnp.float32),
        in_specs=[vmem] * (len(own) + len(other)),
        out_specs=vmem,
        scratch_shapes=[pltpu.VMEM((2, rows, CHUNK), jnp.float32)] * 2,
        compiler_params=pltpu.CompilerParams(vmem_limit_bytes=20 * 1024 * 1024),
        cost_estimate=pl.CostEstimate(
            flops=2 * work * (ds + dt), bytes_accessed=8 * rows * (ds + dt), transcendentals=2 * work
        ),
    )(*own, *other)


def late_kernel(ds, dt, units, known, *refs):
    own, other = refs[:units], refs[units : 2 * units]
    before, out, l, g, ls, gs, stats = refs[2 * units :]
    rows = total_rows(own)
    chunks = rows // CHUNK
    done = known // CHUNK
    line, xi = where_am_i()

    def lanes(j):
        return j * CHUNK, (j + 1) * CHUNK

    for j in range(done):
        products(ds, dt, own, other, lanes(j), (known, rows), ls.at[j], gs.at[j])
    for j in range(done, chunks):
        products(ds, dt, own, other, lanes(j), (0, rows), l.at[j % 2], g.at[j % 2])
        if j == done:
            for i in range(done):
                to = slice(*lanes(i))
                lse, mark, mean, _ = summary(ds, dt, ls.at[i], gs.at[i], rows - known, False)
                old_lse, old_mark, old_mean = (before[n : n + 1, to] for n in range(3))
                top = jnp.maximum(lse, old_lse)
                stats[0:1, to] = top + jnp.log(jnp.exp(lse - top) + jnp.exp(old_lse - top))
                top = jnp.maximum(mark, old_mark)
                one, two = jnp.exp(mark - top), jnp.exp(old_mark - top)
                stats[1:2, to] = top + jnp.log(one + two)
                stats[2:3, to] = (one * mean + two * old_mean) / (one + two)
                stats[3:4, to] = before[3:4, to]
        else:
            for n, v in enumerate(summary(ds, dt, l.at[(j - 1) % 2], g.at[(j - 1) % 2], rows, False)):
                stats[n : n + 1, slice(*lanes(j - 1))] = v
    for n, v in enumerate(summary(ds, dt, l.at[(chunks - 1) % 2], g.at[(chunks - 1) % 2], rows, False)):
        stats[n : n + 1, slice(*lanes(chunks - 1))] = v

    places = {}
    at = 0
    for steps, partner in ORDER:
        for step in steps:
            places[step, partner] = at
            at += 2 * SHARD
    for step in range(8):
        mine, across = (stats[:4, places[step, p] : places[step, p] + 2 * SHARD] for p in (0, 1))
        v = jnp.concatenate([jnp.where(xi == 0, mine, across), jnp.where(xi == 0, across, mine)], axis=1)
        row = pl.ds(lax.rem(line + step, 8), 1)
        for n in range(4):
            out[0, n, row, :] = v[n : n + 1, :128]
            out[0, 4 + n // 2, row, (n % 2) * 64 : (n % 2 + 1) * 64] = v[n : n + 1, 128:]
    for k in range(1, out.shape[0]):
        out[k] = out[0]


def late(own, other, before, known, ds, dt):
    rows = total_rows(own)
    chunks, done = rows // CHUNK, known // CHUNK
    vmem = pl.BlockSpec(memory_space=pltpu.VMEM)
    work = rows * rows - known * done * CHUNK
    return pl.pallas_call(
        functools.partial(late_kernel, ds, dt, len(own), known),
        out_shape=jax.ShapeDtypeStruct((16, 6, 8, 128), jnp.float32),
        in_specs=[vmem] * (len(own) + len(other) + 1),
        out_specs=vmem,
        scratch_shapes=[pltpu.VMEM((2, rows, CHUNK), jnp.float32)] * 2
        + [pltpu.VMEM((done, rows - known, CHUNK), jnp.float32)] * 2
        + [pltpu.VMEM((8, rows), jnp.float32)],
        compiler_params=pltpu.CompilerParams(vmem_limit_bytes=20 * 1024 * 1024),
        cost_estimate=pl.CostEstimate(
            flops=2 * work * (ds + dt), bytes_accessed=8 * rows * (ds + dt), transcendentals=2 * work
        ),
    )(*own, *other, before)


def losses(parts, count, lse, mark, mean, diagonal):
    top, high = lse(0), mark(0)
    for k in range(1, count):
        top = jnp.maximum(top, lse(k))
        high = jnp.maximum(high, mark(k))
    spread = mass = weighted = own = jnp.zeros_like(top)
    for k in range(count):
        e = jnp.exp(mark(k) - high)
        spread += jnp.exp(lse(k) - top)
        mass += e
        weighted += e * mean(k)
        own += diagonal(k)
    return top + jnp.log(spread) - 0.5 * own - 0.5 * weighted / mass


def halves(parts, rows):
    count = parts.shape[0]
    return (
        losses(parts, count, *(lambda k, n=n: parts[k, n, rows, :] for n in range(4))),
        losses(
            parts,
            count,
            *(lambda k, n=n: parts[k, 4 + n // 2, rows, (n % 2) * 64 : (n % 2 + 1) * 64] for n in range(4)),
        ),
    )


def finish_kernel(parts, mine, total, held):
    line, xi = where_am_i()
    one, two = halves(parts, slice(0, 8))
    held[:, :128] = one
    held[:, 128:] = jnp.concatenate([two, two], axis=1)
    v = held[pl.ds(line, 1), :]
    mine[...] = jnp.where(xi == 0, v[:, :128], v[:, 2 * SHARD : 2 * SHARD + 128])
    total[...] = jnp.full(total.shape, jnp.sum(one) + jnp.sum(two), jnp.float32)


def finish(parts):
    vmem = pl.BlockSpec(memory_space=pltpu.VMEM)
    return pl.pallas_call(
        finish_kernel,
        out_shape=(
            jax.ShapeDtypeStruct((1, 128), jnp.float32),
            jax.ShapeDtypeStruct((32, 1, 128), jnp.float32),
        ),
        in_specs=[vmem],
        out_specs=[vmem] * 2,
        scratch_shapes=[pltpu.VMEM((8, 256), jnp.float32)],
        compiler_params=pltpu.CompilerParams(vmem_limit_bytes=4 * 1024 * 1024),
    )(parts)


def shards(image_student, text_student, image_teacher, text_teacher):
    ds, dt = image_student.shape[1], image_teacher.shape[1]
    core = lax.axis_index("img") % 2

    def swap(v):
        return lax.ppermute(v, AXES, CORE_PAIRS)

    mine, theirs = pack(image_student, text_student, image_teacher, text_teacher)
    def pass_on(v):
        return lax.ppermute(v, AXES, X_PAIRS)

    def joined(*v):
        return jnp.concatenate(v, axis=0)

    def after(v, *others):
        return lax.optimization_barrier((v, others))[0]

    chip = joined(mine, swap(theirs))
    up, down = [chip], [chip]
    for _ in range(3):
        up.append(lax.ppermute(up[-1], AXES, UP))
        down.append(lax.ppermute(down[-1], AXES, DOWN))
    near = joined(chip, up[1], down[1])
    near_across = pass_on(near)
    middle = after(joined(up[2], down[2]), near_across)
    middle_across = pass_on(middle)
    last = lax.ppermute(up[3], AXES, UP)
    end = after(joined(up[3], down[3], last), middle_across)
    end_across = pass_on(end)
    own = [near, near_across, middle, middle_across]
    known = total_rows(own)
    other = [swap(v) for v in own]
    before = early(own, other, ds, dt)
    end_other = swap(end)
    own += [end, end_across]
    other += [end_other, swap(after(end_across, before, end_other))]
    stats = late(own, other, before, known, ds, dt)
    parts = lax.all_to_all(stats, AXES, 0, 0, axis_index_groups=STAT_GROUPS)
    chip, total = finish(parts)
    first, second = chip[0, :SHARD], swap(chip)[0, SHARD : 2 * SHARD]
    image_loss = jnp.where(core == 0, first, second)
    text_loss = jnp.where(core == 0, second, first)
    totals = lax.all_to_all(total, AXES, 0, 0, axis_index_groups=SUM_GROUPS)
    return image_loss, text_loss, jnp.sum(totals[:, 0, 0]) / (2.0 * SHARD * 512)


def solution(mesh):
    spec = P(("img", "txt"), None)
    return jax.shard_map(
        shards,
        mesh=mesh,
        in_specs=(spec, spec, spec, spec),
        out_specs=(P(("img", "txt")), P(("img", "txt")), P()),
        check_vma=False,
    )
```

```python
import functools
import math

import jax
import jax.numpy as jnp
from jax import lax
from jax.experimental import pallas as pl
from jax.experimental.pallas import tpu as pltpu
from jax.sharding import PartitionSpec as P

AXES = ("img", "txt")
LOG2E = 1.0 / math.log(2.0)
LOW = -1e30
SHARD = 48
CHUNK = 256
BLOCK = 128
ORDER = (((0, 7, 1), 0), ((0, 7, 1), 1), ((6, 2), 0), ((6, 2), 1), ((5, 3, 4), 0), ((5, 3, 4), 1))


def place(x, y, z, c):
    return (((x // 2) * 8 + y) * 2 + c) * 16 + z * 2 + x % 2


def everywhere():
    return [
        (x, y, z, c) for x in range(4) for y in range(8) for z in range(8) for c in range(2)
    ]


ROW_X = ((0, 1), (3, 2))
COL_X = ((0, 3), (1, 2))
CORE_PAIRS = [(place(x, y, z, c), place(x, y, z, 1 - c)) for x, y, z, c in everywhere()]
X_PAIRS = [
    (place(x, y, z, c), place(x ^ 1 if c == 0 else 3 - x, y, z, c)) for x, y, z, c in everywhere()
]
UP, DOWN = (
    [
        (place(x, y, z, c), place(x, y, (z + s) % 8, c) if c == 0 else place(x, (y + s) % 8, z, c))
        for x, y, z, c in everywhere()
    ]
    for s in (1, -1)
)
STAT_GROUPS = [[place(x, y, z, 0) for z in range(8) for x in pair] for pair in ROW_X for y in range(8)] + [
    [place(x, y, z, 1) for y in range(8) for x in pair] for pair in COL_X for z in range(8)
]
SUM_GROUPS = [
    [place(pair[e], y, k, 0) for y in range(8) for pair in ROW_X]
    + [place(pair[e], k, z, 1) for z in range(8) for pair in COL_X]
    for k in range(8)
    for e in range(2)
]


def where_am_i():
    img = lax.axis_index("img")
    txt = lax.axis_index("txt")
    x_hi, x_lo = img // 16, txt % 2
    core = img % 2
    return jnp.where(core == 0, txt // 2, (img // 2) % 8), jnp.where(core == 0, x_hi ^ x_lo, x_hi)


def dot(left, right):
    return lax.dot_general(
        left, right, (((1,), (1,)), ((), ())), preferred_element_type=jnp.float32
    )


def pack_kernel(image_s, text_s, image_t, text_t, mine, theirs, sems):
    ds, dt = image_s.shape[1], image_t.shape[1]
    core = lax.axis_index("img") % 2

    def copies(image_out, text_out):
        parts = (pl.ds(0, ds), pl.ds(ds, dt), pl.ds(ds + dt, dt))
        out = []
        for n, source in enumerate((image_s, image_t, text_t)):
            out.append(pltpu.make_async_copy(source, image_out.at[:, parts[n]], sems.at[n]))
        for n, source in enumerate((text_s, text_t, image_t)):
            out.append(pltpu.make_async_copy(source, text_out.at[:, parts[n]], sems.at[3 + n]))
        return out

    @pl.when(core == 0)
    def _():
        for copy in copies(mine, theirs):
            copy.start()

    @pl.when(core == 1)
    def _():
        for copy in copies(theirs, mine):
            copy.start()

    for copy in copies(mine, theirs):
        copy.wait()


def pack(image_s, text_s, image_t, text_t):
    shape = jax.ShapeDtypeStruct((SHARD, image_s.shape[1] + 2 * image_t.shape[1]), jnp.bfloat16)
    return pl.pallas_call(
        pack_kernel,
        out_shape=(shape, shape),
        in_specs=[pl.BlockSpec(memory_space=pl.ANY)] * 4,
        out_specs=[pl.BlockSpec(memory_space=pltpu.VMEM)] * 2,
        scratch_shapes=[pltpu.SemaphoreType.DMA((6,))],
        compiler_params=pltpu.CompilerParams(vmem_limit_bytes=60 * 1024 * 1024),
    )(image_s, text_s, image_t, text_t)


def total_rows(refs):
    return sum(ref.shape[0] for ref in refs)


def piece(refs, start, stop, low, high):
    parts, at = [], 0
    for ref in refs:
        size = ref.shape[0]
        a, b = max(start - at, 0), min(stop - at, size)
        if a < b:
            parts.append(ref[a:b, low:high])
        at += size
    return jnp.concatenate(parts, axis=0) if len(parts) > 1 else parts[0]


def products(ds, dt, own, other, lanes, rows, l, g):
    l[: rows[1] - rows[0], :] = dot(piece(other, *rows, 0, ds), piece(own, *lanes, 0, ds))
    g[: rows[1] - rows[0], :] = dot(piece(other, *rows, ds + dt, ds + 2 * dt), piece(own, *lanes, ds, ds + dt))


def summary(ds, dt, l, g, rows, first):
    kl = 2.0 / math.sqrt(ds) * LOG2E
    kt = 3.0 / math.sqrt(dt) * LOG2E
    diagonal = jnp.zeros((1, CHUNK), jnp.float32)
    if first:
        s = lax.broadcasted_iota(jnp.int32, (2 * SHARD, CHUNK), 0)
        r = lax.broadcasted_iota(jnp.int32, (2 * SHARD, CHUNK), 1)
        same = (r < 2 * SHARD) & (s == jnp.where(r < SHARD, r + SHARD, r - SHARD))
        g[: 2 * SHARD, :] = jnp.where(same, LOW, g[: 2 * SHARD, :])
        diagonal = jnp.sum(jnp.where(same, l[: 2 * SHARD, :], 0.0), axis=0, keepdims=True)
    blocks = [slice(i, min(i + BLOCK, rows)) for i in range(0, rows, BLOCK)]

    def eights(v):
        return v.reshape(v.shape[0] // 8, 8, CHUNK)

    top = high = jnp.full((8, CHUNK), LOW, jnp.float32)
    for here in blocks:
        top = jnp.maximum(top, jnp.max(eights(l[here, :]), axis=0))
        high = jnp.maximum(high, jnp.max(eights(g[here, :]), axis=0))
    top = jnp.max(top, axis=0, keepdims=True)
    high = jnp.max(high, axis=0, keepdims=True)
    total = mass = weighted = jnp.zeros((8, CHUNK), jnp.float32)
    for here in blocks:
        lv = l[here, :]
        e = jnp.exp2((g[here, :] - high) * kt)
        total += jnp.sum(eights(jnp.exp2((lv - top) * kl)), axis=0)
        mass += jnp.sum(eights(e), axis=0)
        weighted += jnp.sum(eights(e * lv), axis=0)
    total = jnp.sum(total, axis=0, keepdims=True)
    mass = jnp.sum(mass, axis=0, keepdims=True)
    weighted = jnp.sum(weighted, axis=0, keepdims=True)
    return (
        top * (kl / LOG2E) + jnp.log(total),
        high * (kt / LOG2E) + jnp.log(mass),
        weighted / mass * (kl / LOG2E),
        diagonal * (kl / LOG2E),
    )


def early_kernel(ds, dt, units, *refs):
    own, other = refs[:units], refs[units : 2 * units]
    out, l, g = refs[2 * units :]
    rows = total_rows(own)
    chunks = rows // CHUNK

    def multiply(j):
        products(ds, dt, own, other, (j * CHUNK, (j + 1) * CHUNK), (0, rows), l.at[j % 2], g.at[j % 2])

    multiply(0)
    for j in range(chunks):
        if j + 1 < chunks:
            multiply(j + 1)
        for n, v in enumerate(summary(ds, dt, l.at[j % 2], g.at[j % 2], rows, j == 0)):
            out[n : n + 1, j * CHUNK : (j + 1) * CHUNK] = v


def early(own, other, ds, dt):
    rows = total_rows(own)
    chunks = rows // CHUNK
    vmem = pl.BlockSpec(memory_space=pltpu.VMEM)
    work = rows * chunks * CHUNK
    return pl.pallas_call(
        functools.partial(early_kernel, ds, dt, len(own)),
        out_shape=jax.ShapeDtypeStruct((8, chunks * CHUNK), jnp.float32),
        in_specs=[vmem] * (len(own) + len(other)),
        out_specs=vmem,
        scratch_shapes=[pltpu.VMEM((2, rows, CHUNK), jnp.float32)] * 2,
        compiler_params=pltpu.CompilerParams(vmem_limit_bytes=20 * 1024 * 1024),
        cost_estimate=pl.CostEstimate(
            flops=2 * work * (ds + dt), bytes_accessed=8 * rows * (ds + dt), transcendentals=2 * work
        ),
    )(*own, *other)


def late_kernel(ds, dt, units, known, *refs):
    own, other = refs[:units], refs[units : 2 * units]
    before, out, l, g, ls, gs, stats = refs[2 * units :]
    rows = total_rows(own)
    chunks = rows // CHUNK
    done = known // CHUNK
    line, xi = where_am_i()

    def lanes(j):
        return j * CHUNK, (j + 1) * CHUNK

    for j in range(done):
        products(ds, dt, own, other, lanes(j), (known, rows), ls.at[j], gs.at[j])
    for j in range(done, chunks):
        products(ds, dt, own, other, lanes(j), (0, rows), l.at[j % 2], g.at[j % 2])
        if j == done:
            for i in range(done):
                to = slice(*lanes(i))
                lse, mark, mean, _ = summary(ds, dt, ls.at[i], gs.at[i], rows - known, False)
                old_lse, old_mark, old_mean = (before[n : n + 1, to] for n in range(3))
                top = jnp.maximum(lse, old_lse)
                stats[0:1, to] = top + jnp.log(jnp.exp(lse - top) + jnp.exp(old_lse - top))
                top = jnp.maximum(mark, old_mark)
                one, two = jnp.exp(mark - top), jnp.exp(old_mark - top)
                stats[1:2, to] = top + jnp.log(one + two)
                stats[2:3, to] = (one * mean + two * old_mean) / (one + two)
                stats[3:4, to] = before[3:4, to]
        else:
            for n, v in enumerate(summary(ds, dt, l.at[(j - 1) % 2], g.at[(j - 1) % 2], rows, False)):
                stats[n : n + 1, slice(*lanes(j - 1))] = v
    for n, v in enumerate(summary(ds, dt, l.at[(chunks - 1) % 2], g.at[(chunks - 1) % 2], rows, False)):
        stats[n : n + 1, slice(*lanes(chunks - 1))] = v

    places = {}
    at = 0
    for steps, partner in ORDER:
        for step in steps:
            places[step, partner] = at
            at += 2 * SHARD
    for step in range(8):
        mine, across = (stats[:4, places[step, p] : places[step, p] + 2 * SHARD] for p in (0, 1))
        v = jnp.concatenate([jnp.where(xi == 0, mine, across), jnp.where(xi == 0, across, mine)], axis=1)
        row = pl.ds(lax.rem(line + step, 8), 1)
        for n in range(4):
            out[0, n, row, :] = v[n : n + 1, :128]
            out[0, 4 + n // 2, row, (n % 2) * 64 : (n % 2 + 1) * 64] = v[n : n + 1, 128:]
    for k in range(1, out.shape[0]):
        out[k] = out[0]


def late(own, other, before, known, ds, dt):
    rows = total_rows(own)
    chunks, done = rows // CHUNK, known // CHUNK
    vmem = pl.BlockSpec(memory_space=pltpu.VMEM)
    work = rows * rows - known * done * CHUNK
    return pl.pallas_call(
        functools.partial(late_kernel, ds, dt, len(own), known),
        out_shape=jax.ShapeDtypeStruct((16, 6, 8, 128), jnp.float32),
        in_specs=[vmem] * (len(own) + len(other) + 1),
        out_specs=vmem,
        scratch_shapes=[pltpu.VMEM((2, rows, CHUNK), jnp.float32)] * 2
        + [pltpu.VMEM((done, rows - known, CHUNK), jnp.float32)] * 2
        + [pltpu.VMEM((8, rows), jnp.float32)],
        compiler_params=pltpu.CompilerParams(vmem_limit_bytes=20 * 1024 * 1024),
        cost_estimate=pl.CostEstimate(
            flops=2 * work * (ds + dt), bytes_accessed=8 * rows * (ds + dt), transcendentals=2 * work
        ),
    )(*own, *other, before)


def losses(parts, count, lse, mark, mean, diagonal):
    top, high = lse(0), mark(0)
    for k in range(1, count):
        top = jnp.maximum(top, lse(k))
        high = jnp.maximum(high, mark(k))
    spread = mass = weighted = own = jnp.zeros_like(top)
    for k in range(count):
        e = jnp.exp(mark(k) - high)
        spread += jnp.exp(lse(k) - top)
        mass += e
        weighted += e * mean(k)
        own += diagonal(k)
    return top + jnp.log(spread) - 0.5 * own - 0.5 * weighted / mass


def halves(parts, rows):
    count = parts.shape[0]
    return (
        losses(parts, count, *(lambda k, n=n: parts[k, n, rows, :] for n in range(4))),
        losses(
            parts,
            count,
            *(lambda k, n=n: parts[k, 4 + n // 2, rows, (n % 2) * 64 : (n % 2 + 1) * 64] for n in range(4)),
        ),
    )


def finish_kernel(parts, mine, total, held):
    line, xi = where_am_i()
    one, two = halves(parts, slice(0, 8))
    held[:, :128] = one
    held[:, 128:] = jnp.concatenate([two, two], axis=1)
    v = held[pl.ds(line, 1), :]
    mine[...] = jnp.where(xi == 0, v[:, :128], v[:, 2 * SHARD : 2 * SHARD + 128])
    total[...] = jnp.full(total.shape, jnp.sum(one) + jnp.sum(two), jnp.float32)


def finish(parts):
    vmem = pl.BlockSpec(memory_space=pltpu.VMEM)
    return pl.pallas_call(
        finish_kernel,
        out_shape=(
            jax.ShapeDtypeStruct((1, 128), jnp.float32),
            jax.ShapeDtypeStruct((32, 1, 128), jnp.float32),
        ),
        in_specs=[vmem],
        out_specs=[vmem] * 2,
        scratch_shapes=[pltpu.VMEM((8, 256), jnp.float32)],
        compiler_params=pltpu.CompilerParams(vmem_limit_bytes=4 * 1024 * 1024),
    )(parts)


def shards(image_student, text_student, image_teacher, text_teacher):
    ds, dt = image_student.shape[1], image_teacher.shape[1]
    core = lax.axis_index("img") % 2

    def swap(v):
        return lax.ppermute(v, AXES, CORE_PAIRS)

    mine, theirs = pack(image_student, text_student, image_teacher, text_teacher)
    def pass_on(v):
        return lax.ppermute(v, AXES, X_PAIRS)

    def joined(*v):
        return jnp.concatenate(v, axis=0)

    def after(v, *others):
        return lax.optimization_barrier((v, others))[0]

    chip = joined(mine, swap(theirs))
    up, down = [chip], [chip]
    for _ in range(3):
        up.append(lax.ppermute(up[-1], AXES, UP))
        down.append(lax.ppermute(down[-1], AXES, DOWN))
    near = joined(chip, up[1], down[1])
    near_across = pass_on(near)
    middle = joined(up[2], down[2])
    middle_across = pass_on(middle)
    last = lax.ppermute(up[3], AXES, UP)
    end = after(joined(up[3], down[3], last), near_across, middle_across)
    end_across = pass_on(end)
    own = [near, near_across, middle, middle_across]
    known = total_rows(own)
    other = [swap(v) for v in own]
    before = early(own, other, ds, dt)
    end_other = swap(end)
    own += [end, end_across]
    other += [end_other, swap(after(end_across, before, end_other))]
    stats = late(own, other, before, known, ds, dt)
    parts = lax.all_to_all(stats, AXES, 0, 0, axis_index_groups=STAT_GROUPS)
    chip, total = finish(parts)
    first, second = chip[0, :SHARD], swap(chip)[0, SHARD : 2 * SHARD]
    image_loss = jnp.where(core == 0, first, second)
    text_loss = jnp.where(core == 0, second, first)
    totals = lax.all_to_all(total, AXES, 0, 0, axis_index_groups=SUM_GROUPS)
    return image_loss, text_loss, jnp.sum(totals[:, 0, 0]) / (2.0 * SHARD * 512)


def solution(mesh):
    spec = P(("img", "txt"), None)
    return jax.shard_map(
        shards,
        mesh=mesh,
        in_specs=(spec, spec, spec, spec),
        out_specs=(P(("img", "txt")), P(("img", "txt")), P()),
        check_vma=False,
    )
```

```python
import functools
import math

import jax
import jax.numpy as jnp
from jax import lax
from jax.experimental import pallas as pl
from jax.experimental.pallas import tpu as pltpu
from jax.sharding import PartitionSpec as P

AXES = ("img", "txt")
LOG2E = 1.0 / math.log(2.0)
LOW = -1e30
SHARD = 48
CHUNK = 256
BLOCK = 128
ORDER = (((0, 7, 1), 0), ((0, 7, 1), 1), ((6, 2), 0), ((6, 2), 1), ((5, 3, 4), 0), ((5, 3, 4), 1))


def place(x, y, z, c):
    return (((x // 2) * 8 + y) * 2 + c) * 16 + z * 2 + x % 2


def everywhere():
    return [
        (x, y, z, c) for x in range(4) for y in range(8) for z in range(8) for c in range(2)
    ]


ROW_X = ((0, 1), (3, 2))
COL_X = ((0, 3), (1, 2))
CORE_PAIRS = [(place(x, y, z, c), place(x, y, z, 1 - c)) for x, y, z, c in everywhere()]
X_PAIRS = [
    (place(x, y, z, c), place(x ^ 1 if c == 0 else 3 - x, y, z, c)) for x, y, z, c in everywhere()
]
UP, DOWN = (
    [
        (place(x, y, z, c), place(x, y, (z + s) % 8, c) if c == 0 else place(x, (y + s) % 8, z, c))
        for x, y, z, c in everywhere()
    ]
    for s in (1, -1)
)
STAT_GROUPS = [[place(x, y, z, 0) for z in range(8) for x in pair] for pair in ROW_X for y in range(8)] + [
    [place(x, y, z, 1) for y in range(8) for x in pair] for pair in COL_X for z in range(8)
]
SUM_GROUPS = [
    [place(pair[e], y, k, 0) for y in range(8) for pair in ROW_X]
    + [place(pair[e], k, z, 1) for z in range(8) for pair in COL_X]
    for k in range(8)
    for e in range(2)
]


def where_am_i():
    img = lax.axis_index("img")
    txt = lax.axis_index("txt")
    x_hi, x_lo = img // 16, txt % 2
    core = img % 2
    return jnp.where(core == 0, txt // 2, (img // 2) % 8), jnp.where(core == 0, x_hi ^ x_lo, x_hi)


def dot(left, right):
    return lax.dot_general(
        left, right, (((1,), (1,)), ((), ())), preferred_element_type=jnp.float32
    )


def pack_kernel(image_s, text_s, image_t, text_t, mine, theirs, sems):
    ds, dt = image_s.shape[1], image_t.shape[1]
    core = lax.axis_index("img") % 2

    def copies(image_out, text_out):
        parts = (pl.ds(0, ds), pl.ds(ds, dt), pl.ds(ds + dt, dt))
        out = []
        for n, source in enumerate((image_s, image_t, text_t)):
            out.append(pltpu.make_async_copy(source, image_out.at[:, parts[n]], sems.at[n]))
        for n, source in enumerate((text_s, text_t, image_t)):
            out.append(pltpu.make_async_copy(source, text_out.at[:, parts[n]], sems.at[3 + n]))
        return out

    @pl.when(core == 0)
    def _():
        for copy in copies(mine, theirs):
            copy.start()

    @pl.when(core == 1)
    def _():
        for copy in copies(theirs, mine):
            copy.start()

    for copy in copies(mine, theirs):
        copy.wait()


def pack(image_s, text_s, image_t, text_t):
    shape = jax.ShapeDtypeStruct((SHARD, image_s.shape[1] + 2 * image_t.shape[1]), jnp.bfloat16)
    return pl.pallas_call(
        pack_kernel,
        out_shape=(shape, shape),
        in_specs=[pl.BlockSpec(memory_space=pl.ANY)] * 4,
        out_specs=[pl.BlockSpec(memory_space=pltpu.VMEM)] * 2,
        scratch_shapes=[pltpu.SemaphoreType.DMA((6,))],
        compiler_params=pltpu.CompilerParams(vmem_limit_bytes=60 * 1024 * 1024),
    )(image_s, text_s, image_t, text_t)


def total_rows(refs):
    return sum(ref.shape[0] for ref in refs)


def piece(refs, start, stop, low, high):
    parts, at = [], 0
    for ref in refs:
        size = ref.shape[0]
        a, b = max(start - at, 0), min(stop - at, size)
        if a < b:
            parts.append(ref[a:b, low:high])
        at += size
    return jnp.concatenate(parts, axis=0) if len(parts) > 1 else parts[0]


def products(ds, dt, own, other, lanes, rows, l, g):
    l[: rows[1] - rows[0], :] = dot(piece(other, *rows, 0, ds), piece(own, *lanes, 0, ds))
    g[: rows[1] - rows[0], :] = dot(piece(other, *rows, ds + dt, ds + 2 * dt), piece(own, *lanes, ds, ds + dt))


def summary(ds, dt, l, g, rows, first):
    kl = 2.0 / math.sqrt(ds) * LOG2E
    kt = 3.0 / math.sqrt(dt) * LOG2E
    diagonal = jnp.zeros((1, CHUNK), jnp.float32)
    if first:
        s = lax.broadcasted_iota(jnp.int32, (2 * SHARD, CHUNK), 0)
        r = lax.broadcasted_iota(jnp.int32, (2 * SHARD, CHUNK), 1)
        same = (r < 2 * SHARD) & (s == jnp.where(r < SHARD, r + SHARD, r - SHARD))
        g[: 2 * SHARD, :] = jnp.where(same, LOW, g[: 2 * SHARD, :])
        diagonal = jnp.sum(jnp.where(same, l[: 2 * SHARD, :], 0.0), axis=0, keepdims=True)
    blocks = [slice(i, min(i + BLOCK, rows)) for i in range(0, rows, BLOCK)]

    def eights(v):
        return v.reshape(v.shape[0] // 8, 8, CHUNK)

    top = high = jnp.full((8, CHUNK), LOW, jnp.float32)
    for here in blocks:
        top = jnp.maximum(top, jnp.max(eights(l[here, :]), axis=0))
        high = jnp.maximum(high, jnp.max(eights(g[here, :]), axis=0))
    top = jnp.max(top, axis=0, keepdims=True)
    high = jnp.max(high, axis=0, keepdims=True)
    total = mass = weighted = jnp.zeros((8, CHUNK), jnp.float32)
    for here in blocks:
        lv = l[here, :]
        e = jnp.exp2((g[here, :] - high) * kt)
        total += jnp.sum(eights(jnp.exp2((lv - top) * kl)), axis=0)
        mass += jnp.sum(eights(e), axis=0)
        weighted += jnp.sum(eights(e * lv), axis=0)
    total = jnp.sum(total, axis=0, keepdims=True)
    mass = jnp.sum(mass, axis=0, keepdims=True)
    weighted = jnp.sum(weighted, axis=0, keepdims=True)
    return (
        top * (kl / LOG2E) + jnp.log(total),
        high * (kt / LOG2E) + jnp.log(mass),
        weighted / mass * (kl / LOG2E),
        diagonal * (kl / LOG2E),
    )


def early_kernel(ds, dt, units, *refs):
    own, other = refs[:units], refs[units : 2 * units]
    out, l, g = refs[2 * units :]
    rows = total_rows(own)
    chunks = rows // CHUNK

    def multiply(j):
        products(ds, dt, own, other, (j * CHUNK, (j + 1) * CHUNK), (0, rows), l.at[j % 2], g.at[j % 2])

    multiply(0)
    for j in range(chunks):
        if j + 1 < chunks:
            multiply(j + 1)
        for n, v in enumerate(summary(ds, dt, l.at[j % 2], g.at[j % 2], rows, j == 0)):
            out[n : n + 1, j * CHUNK : (j + 1) * CHUNK] = v


def early(own, other, ds, dt):
    rows = total_rows(own)
    chunks = rows // CHUNK
    vmem = pl.BlockSpec(memory_space=pltpu.VMEM)
    work = rows * chunks * CHUNK
    return pl.pallas_call(
        functools.partial(early_kernel, ds, dt, len(own)),
        out_shape=jax.ShapeDtypeStruct((8, chunks * CHUNK), jnp.float32),
        in_specs=[vmem] * (len(own) + len(other)),
        out_specs=vmem,
        scratch_shapes=[pltpu.VMEM((2, rows, CHUNK), jnp.float32)] * 2,
        compiler_params=pltpu.CompilerParams(vmem_limit_bytes=20 * 1024 * 1024),
        cost_estimate=pl.CostEstimate(
            flops=2 * work * (ds + dt), bytes_accessed=8 * rows * (ds + dt), transcendentals=2 * work
        ),
    )(*own, *other)


def advance(ds, dt, own, other, before, known, stats, l, g, ls, gs):
    rows = total_rows(own)
    chunks = rows // CHUNK
    done = known // CHUNK

    def lanes(j):
        return j * CHUNK, (j + 1) * CHUNK

    for j in range(done):
        products(ds, dt, own, other, lanes(j), (known, rows), ls.at[j], gs.at[j])
    for j in range(done, chunks):
        products(ds, dt, own, other, lanes(j), (0, rows), l.at[j % 2], g.at[j % 2])
        if j == done:
            for i in range(done):
                to = slice(*lanes(i))
                lse, mark, mean, _ = summary(ds, dt, ls.at[i], gs.at[i], rows - known, False)
                old_lse, old_mark, old_mean = (before[n : n + 1, to] for n in range(3))
                top = jnp.maximum(lse, old_lse)
                stats[0:1, to] = top + jnp.log(jnp.exp(lse - top) + jnp.exp(old_lse - top))
                top = jnp.maximum(mark, old_mark)
                one, two = jnp.exp(mark - top), jnp.exp(old_mark - top)
                stats[1:2, to] = top + jnp.log(one + two)
                stats[2:3, to] = (one * mean + two * old_mean) / (one + two)
                stats[3:4, to] = before[3:4, to]
        else:
            for n, v in enumerate(summary(ds, dt, l.at[(j - 1) % 2], g.at[(j - 1) % 2], rows, False)):
                stats[n : n + 1, slice(*lanes(j - 1))] = v
    for n, v in enumerate(summary(ds, dt, l.at[(chunks - 1) % 2], g.at[(chunks - 1) % 2], rows, False)):
        stats[n : n + 1, slice(*lanes(chunks - 1))] = v


def scratch(rows, known):
    return [pltpu.VMEM((2, rows, CHUNK), jnp.float32)] * 2 + [
        pltpu.VMEM((known // CHUNK, rows - known, CHUNK), jnp.float32)
    ] * 2


def between_kernel(ds, dt, units, known, *refs):
    own, other = refs[:units], refs[units : 2 * units]
    before, out, *work = refs[2 * units :]
    advance(ds, dt, own, other, before, known, out, *work)


def between(own, other, before, known, ds, dt):
    rows = total_rows(own)
    lanes = rows // CHUNK * CHUNK
    vmem = pl.BlockSpec(memory_space=pltpu.VMEM)
    work = rows * lanes - known * before.shape[1]
    return pl.pallas_call(
        functools.partial(between_kernel, ds, dt, len(own), known),
        out_shape=jax.ShapeDtypeStruct((8, lanes), jnp.float32),
        in_specs=[vmem] * (len(own) + len(other) + 1),
        out_specs=vmem,
        scratch_shapes=scratch(rows, known),
        compiler_params=pltpu.CompilerParams(vmem_limit_bytes=20 * 1024 * 1024),
        cost_estimate=pl.CostEstimate(
            flops=2 * work * (ds + dt), bytes_accessed=8 * rows * (ds + dt), transcendentals=2 * work
        ),
    )(*own, *other, before)


def late_kernel(ds, dt, units, known, *refs):
    own, other = refs[:units], refs[units : 2 * units]
    before, out, l, g, ls, gs, stats = refs[2 * units :]
    line, xi = where_am_i()
    advance(ds, dt, own, other, before, known, stats, l, g, ls, gs)

    places = {}
    at = 0
    for steps, partner in ORDER:
        for step in steps:
            places[step, partner] = at
            at += 2 * SHARD
    for step in range(8):
        mine, across = (stats[:4, places[step, p] : places[step, p] + 2 * SHARD] for p in (0, 1))
        v = jnp.concatenate([jnp.where(xi == 0, mine, across), jnp.where(xi == 0, across, mine)], axis=1)
        row = pl.ds(lax.rem(line + step, 8), 1)
        for n in range(4):
            out[0, n, row, :] = v[n : n + 1, :128]
            out[0, 4 + n // 2, row, (n % 2) * 64 : (n % 2 + 1) * 64] = v[n : n + 1, 128:]
    for k in range(1, out.shape[0]):
        out[k] = out[0]


def late(own, other, before, known, ds, dt):
    rows = total_rows(own)
    chunks, done = rows // CHUNK, known // CHUNK
    vmem = pl.BlockSpec(memory_space=pltpu.VMEM)
    work = rows * rows - known * done * CHUNK
    return pl.pallas_call(
        functools.partial(late_kernel, ds, dt, len(own), known),
        out_shape=jax.ShapeDtypeStruct((16, 6, 8, 128), jnp.float32),
        in_specs=[vmem] * (len(own) + len(other) + 1),
        out_specs=vmem,
        scratch_shapes=scratch(rows, known) + [pltpu.VMEM((8, rows), jnp.float32)],
        compiler_params=pltpu.CompilerParams(vmem_limit_bytes=20 * 1024 * 1024),
        cost_estimate=pl.CostEstimate(
            flops=2 * work * (ds + dt), bytes_accessed=8 * rows * (ds + dt), transcendentals=2 * work
        ),
    )(*own, *other, before)


def losses(parts, count, lse, mark, mean, diagonal):
    top, high = lse(0), mark(0)
    for k in range(1, count):
        top = jnp.maximum(top, lse(k))
        high = jnp.maximum(high, mark(k))
    spread = mass = weighted = own = jnp.zeros_like(top)
    for k in range(count):
        e = jnp.exp(mark(k) - high)
        spread += jnp.exp(lse(k) - top)
        mass += e
        weighted += e * mean(k)
        own += diagonal(k)
    return top + jnp.log(spread) - 0.5 * own - 0.5 * weighted / mass


def halves(parts, rows):
    count = parts.shape[0]
    return (
        losses(parts, count, *(lambda k, n=n: parts[k, n, rows, :] for n in range(4))),
        losses(
            parts,
            count,
            *(lambda k, n=n: parts[k, 4 + n // 2, rows, (n % 2) * 64 : (n % 2 + 1) * 64] for n in range(4)),
        ),
    )


def finish_kernel(parts, mine, total, held):
    line, xi = where_am_i()
    one, two = halves(parts, slice(0, 8))
    held[:, :128] = one
    held[:, 128:] = jnp.concatenate([two, two], axis=1)
    v = held[pl.ds(line, 1), :]
    mine[...] = jnp.where(xi == 0, v[:, :128], v[:, 2 * SHARD : 2 * SHARD + 128])
    total[...] = jnp.full(total.shape, jnp.sum(one) + jnp.sum(two), jnp.float32)


def finish(parts):
    vmem = pl.BlockSpec(memory_space=pltpu.VMEM)
    return pl.pallas_call(
        finish_kernel,
        out_shape=(
            jax.ShapeDtypeStruct((1, 128), jnp.float32),
            jax.ShapeDtypeStruct((32, 1, 128), jnp.float32),
        ),
        in_specs=[vmem],
        out_specs=[vmem] * 2,
        scratch_shapes=[pltpu.VMEM((8, 256), jnp.float32)],
        compiler_params=pltpu.CompilerParams(vmem_limit_bytes=4 * 1024 * 1024),
    )(parts)


def shards(image_student, text_student, image_teacher, text_teacher):
    ds, dt = image_student.shape[1], image_teacher.shape[1]
    core = lax.axis_index("img") % 2

    def swap(v):
        return lax.ppermute(v, AXES, CORE_PAIRS)

    mine, theirs = pack(image_student, text_student, image_teacher, text_teacher)
    def pass_on(v):
        return lax.ppermute(v, AXES, X_PAIRS)

    def joined(*v):
        return jnp.concatenate(v, axis=0)

    def after(v, *others):
        return lax.optimization_barrier((v, others))[0]

    chip = joined(mine, swap(theirs))
    up, down = [chip], [chip]
    for _ in range(3):
        up.append(lax.ppermute(up[-1], AXES, UP))
        down.append(lax.ppermute(down[-1], AXES, DOWN))
    near = joined(chip, up[1], down[1])
    near_across = pass_on(near)
    middle = joined(up[2], down[2])
    middle_across = pass_on(middle)
    last = lax.ppermute(up[3], AXES, UP)
    end = after(joined(up[3], down[3], last), near_across, middle_across)
    end_across = pass_on(end)
    own = [near, near_across, middle, middle_across]
    known = total_rows(own)
    other = [swap(v) for v in own]
    before = early(own, other, ds, dt)
    end_other = swap(end)
    across_other = swap(after(end_across, before, end_other))
    own.append(end)
    other.append(end_other)
    before = between(own, other, before, known, ds, dt)
    known = total_rows(own)
    stats = late(own + [end_across], other + [across_other], before, known, ds, dt)
    parts = lax.all_to_all(stats, AXES, 0, 0, axis_index_groups=STAT_GROUPS)
    chip, total = finish(parts)
    first, second = chip[0, :SHARD], swap(chip)[0, SHARD : 2 * SHARD]
    image_loss = jnp.where(core == 0, first, second)
    text_loss = jnp.where(core == 0, second, first)
    totals = lax.all_to_all(total, AXES, 0, 0, axis_index_groups=SUM_GROUPS)
    return image_loss, text_loss, jnp.sum(totals[:, 0, 0]) / (2.0 * SHARD * 512)


def solution(mesh):
    spec = P(("img", "txt"), None)
    return jax.shard_map(
        shards,
        mesh=mesh,
        in_specs=(spec, spec, spec, spec),
        out_specs=(P(("img", "txt")), P(("img", "txt")), P()),
        check_vma=False,
    )
```

```python
import functools
import math

import jax
import jax.numpy as jnp
from jax import lax
from jax.experimental import pallas as pl
from jax.experimental.pallas import tpu as pltpu
from jax.sharding import PartitionSpec as P

AXES = ("img", "txt")
LOG2E = 1.0 / math.log(2.0)
LOW = -1e30
SHARD = 48
CHUNK = 256
BLOCK = 128
ORDER = (((0, 7, 1), 0), ((0, 7, 1), 1), ((6, 2), 0), ((6, 2), 1), ((5, 3, 4), 0), ((5, 3, 4), 1))


def place(x, y, z, c):
    return (((x // 2) * 8 + y) * 2 + c) * 16 + z * 2 + x % 2


def everywhere():
    return [
        (x, y, z, c) for x in range(4) for y in range(8) for z in range(8) for c in range(2)
    ]


ROW_X = ((0, 1), (3, 2))
COL_X = ((0, 3), (1, 2))
CORE_PAIRS = [(place(x, y, z, c), place(x, y, z, 1 - c)) for x, y, z, c in everywhere()]
X_PAIRS = [
    (place(x, y, z, c), place(x ^ 1 if c == 0 else 3 - x, y, z, c)) for x, y, z, c in everywhere()
]
UP, DOWN = (
    [
        (place(x, y, z, c), place(x, y, (z + s) % 8, c) if c == 0 else place(x, (y + s) % 8, z, c))
        for x, y, z, c in everywhere()
    ]
    for s in (1, -1)
)
STAT_GROUPS = [[place(x, y, z, 0) for z in range(8) for x in pair] for pair in ROW_X for y in range(8)] + [
    [place(x, y, z, 1) for y in range(8) for x in pair] for pair in COL_X for z in range(8)
]
SUM_GROUPS = [
    [place(pair[e], y, k, 0) for y in range(8) for pair in ROW_X]
    + [place(pair[e], k, z, 1) for z in range(8) for pair in COL_X]
    for k in range(8)
    for e in range(2)
]


def where_am_i():
    img = lax.axis_index("img")
    txt = lax.axis_index("txt")
    x_hi, x_lo = img // 16, txt % 2
    core = img % 2
    return jnp.where(core == 0, txt // 2, (img // 2) % 8), jnp.where(core == 0, x_hi ^ x_lo, x_hi)


def dot(left, right):
    return lax.dot_general(
        left, right, (((1,), (1,)), ((), ())), preferred_element_type=jnp.float32
    )


def pack_kernel(image_s, text_s, image_t, text_t, mine, theirs, sems):
    ds, dt = image_s.shape[1], image_t.shape[1]
    core = lax.axis_index("img") % 2

    def copies(image_out, text_out):
        parts = (pl.ds(0, ds), pl.ds(ds, dt), pl.ds(ds + dt, dt))
        out = []
        for n, source in enumerate((image_s, image_t, text_t)):
            out.append(pltpu.make_async_copy(source, image_out.at[:, parts[n]], sems.at[n]))
        for n, source in enumerate((text_s, text_t, image_t)):
            out.append(pltpu.make_async_copy(source, text_out.at[:, parts[n]], sems.at[3 + n]))
        return out

    @pl.when(core == 0)
    def _():
        for copy in copies(mine, theirs):
            copy.start()

    @pl.when(core == 1)
    def _():
        for copy in copies(theirs, mine):
            copy.start()

    for copy in copies(mine, theirs):
        copy.wait()


def pack(image_s, text_s, image_t, text_t):
    shape = jax.ShapeDtypeStruct((SHARD, image_s.shape[1] + 2 * image_t.shape[1]), jnp.bfloat16)
    return pl.pallas_call(
        pack_kernel,
        out_shape=(shape, shape),
        in_specs=[pl.BlockSpec(memory_space=pl.ANY)] * 4,
        out_specs=[pl.BlockSpec(memory_space=pltpu.VMEM)] * 2,
        scratch_shapes=[pltpu.SemaphoreType.DMA((6,))],
        compiler_params=pltpu.CompilerParams(vmem_limit_bytes=60 * 1024 * 1024),
    )(image_s, text_s, image_t, text_t)


def total_rows(refs):
    return sum(ref.shape[0] for ref in refs)


def piece(refs, start, stop, low, high):
    parts, at = [], 0
    for ref in refs:
        size = ref.shape[0]
        a, b = max(start - at, 0), min(stop - at, size)
        if a < b:
            parts.append(ref[a:b, low:high])
        at += size
    return jnp.concatenate(parts, axis=0) if len(parts) > 1 else parts[0]


def products(ds, dt, own, other, lanes, rows, l, g):
    l[: rows[1] - rows[0], :] = dot(piece(other, *rows, 0, ds), piece(own, *lanes, 0, ds))
    g[: rows[1] - rows[0], :] = dot(piece(other, *rows, ds + dt, ds + 2 * dt), piece(own, *lanes, ds, ds + dt))


def summary(ds, dt, l, g, rows, first):
    kl = 2.0 / math.sqrt(ds) * LOG2E
    kt = 3.0 / math.sqrt(dt) * LOG2E
    diagonal = jnp.zeros((1, CHUNK), jnp.float32)
    if first:
        s = lax.broadcasted_iota(jnp.int32, (2 * SHARD, CHUNK), 0)
        r = lax.broadcasted_iota(jnp.int32, (2 * SHARD, CHUNK), 1)
        same = (r < 2 * SHARD) & (s == jnp.where(r < SHARD, r + SHARD, r - SHARD))
        g[: 2 * SHARD, :] = jnp.where(same, LOW, g[: 2 * SHARD, :])
        diagonal = jnp.sum(jnp.where(same, l[: 2 * SHARD, :], 0.0), axis=0, keepdims=True)
    blocks = [slice(i, min(i + BLOCK, rows)) for i in range(0, rows, BLOCK)]

    def eights(v):
        return v.reshape(v.shape[0] // 8, 8, CHUNK)

    top = high = jnp.full((8, CHUNK), LOW, jnp.float32)
    for here in blocks:
        top = jnp.maximum(top, jnp.max(eights(l[here, :]), axis=0))
        high = jnp.maximum(high, jnp.max(eights(g[here, :]), axis=0))
    top = jnp.max(top, axis=0, keepdims=True)
    high = jnp.max(high, axis=0, keepdims=True)
    total = mass = weighted = jnp.zeros((8, CHUNK), jnp.float32)
    for here in blocks:
        lv = l[here, :]
        e = jnp.exp2((g[here, :] - high) * kt)
        total += jnp.sum(eights(jnp.exp2((lv - top) * kl)), axis=0)
        mass += jnp.sum(eights(e), axis=0)
        weighted += jnp.sum(eights(e * lv), axis=0)
    total = jnp.sum(total, axis=0, keepdims=True)
    mass = jnp.sum(mass, axis=0, keepdims=True)
    weighted = jnp.sum(weighted, axis=0, keepdims=True)
    return (
        top * (kl / LOG2E) + jnp.log(total),
        high * (kt / LOG2E) + jnp.log(mass),
        weighted / mass * (kl / LOG2E),
        diagonal * (kl / LOG2E),
    )


def early_kernel(ds, dt, units, *refs):
    own, other = refs[:units], refs[units : 2 * units]
    out, l, g = refs[2 * units :]
    rows = total_rows(own)
    chunks = rows // CHUNK

    def multiply(j):
        products(ds, dt, own, other, (j * CHUNK, (j + 1) * CHUNK), (0, rows), l.at[j % 2], g.at[j % 2])

    multiply(0)
    for j in range(chunks):
        if j + 1 < chunks:
            multiply(j + 1)
        for n, v in enumerate(summary(ds, dt, l.at[j % 2], g.at[j % 2], rows, j == 0)):
            out[n : n + 1, j * CHUNK : (j + 1) * CHUNK] = v


def early(own, other, ds, dt):
    rows = total_rows(own)
    chunks = rows // CHUNK
    vmem = pl.BlockSpec(memory_space=pltpu.VMEM)
    work = rows * chunks * CHUNK
    return pl.pallas_call(
        functools.partial(early_kernel, ds, dt, len(own)),
        out_shape=jax.ShapeDtypeStruct((8, chunks * CHUNK), jnp.float32),
        in_specs=[vmem] * (len(own) + len(other)),
        out_specs=vmem,
        scratch_shapes=[pltpu.VMEM((2, rows, CHUNK), jnp.float32)] * 2,
        compiler_params=pltpu.CompilerParams(vmem_limit_bytes=20 * 1024 * 1024),
        cost_estimate=pl.CostEstimate(
            flops=2 * work * (ds + dt), bytes_accessed=8 * rows * (ds + dt), transcendentals=2 * work
        ),
    )(*own, *other)


def advance(ds, dt, own, other, before, known, stats, l, g, ls, gs):
    rows = total_rows(own)
    chunks = rows // CHUNK
    done = known // CHUNK

    def lanes(j):
        return j * CHUNK, (j + 1) * CHUNK

    for j in range(done):
        products(ds, dt, own, other, lanes(j), (known, rows), ls.at[j], gs.at[j])
    for j in range(done, chunks):
        products(ds, dt, own, other, lanes(j), (0, rows), l.at[j % 2], g.at[j % 2])
        if j == done:
            for i in range(done):
                to = slice(*lanes(i))
                lse, mark, mean, _ = summary(ds, dt, ls.at[i], gs.at[i], rows - known, False)
                old_lse, old_mark, old_mean = (before[n : n + 1, to] for n in range(3))
                top = jnp.maximum(lse, old_lse)
                stats[0:1, to] = top + jnp.log(jnp.exp(lse - top) + jnp.exp(old_lse - top))
                top = jnp.maximum(mark, old_mark)
                one, two = jnp.exp(mark - top), jnp.exp(old_mark - top)
                stats[1:2, to] = top + jnp.log(one + two)
                stats[2:3, to] = (one * mean + two * old_mean) / (one + two)
                stats[3:4, to] = before[3:4, to]
        else:
            for n, v in enumerate(summary(ds, dt, l.at[(j - 1) % 2], g.at[(j - 1) % 2], rows, False)):
                stats[n : n + 1, slice(*lanes(j - 1))] = v
    for n, v in enumerate(summary(ds, dt, l.at[(chunks - 1) % 2], g.at[(chunks - 1) % 2], rows, False)):
        stats[n : n + 1, slice(*lanes(chunks - 1))] = v


def scratch(rows, known):
    return [pltpu.VMEM((2, rows, CHUNK), jnp.float32)] * 2 + [
        pltpu.VMEM((known // CHUNK, rows - known, CHUNK), jnp.float32)
    ] * 2


def between_kernel(ds, dt, units, known, *refs):
    own, other = refs[:units], refs[units : 2 * units]
    before, out, *work = refs[2 * units :]
    advance(ds, dt, own, other, before, known, out, *work)


def between(own, other, before, known, ds, dt):
    rows = total_rows(own)
    lanes = rows // CHUNK * CHUNK
    vmem = pl.BlockSpec(memory_space=pltpu.VMEM)
    work = rows * lanes - known * before.shape[1]
    return pl.pallas_call(
        functools.partial(between_kernel, ds, dt, len(own), known),
        out_shape=jax.ShapeDtypeStruct((8, lanes), jnp.float32),
        in_specs=[vmem] * (len(own) + len(other) + 1),
        out_specs=vmem,
        scratch_shapes=scratch(rows, known),
        compiler_params=pltpu.CompilerParams(vmem_limit_bytes=20 * 1024 * 1024),
        cost_estimate=pl.CostEstimate(
            flops=2 * work * (ds + dt), bytes_accessed=8 * rows * (ds + dt), transcendentals=2 * work
        ),
    )(*own, *other, before)


def late_kernel(ds, dt, units, known, *refs):
    own, other = refs[:units], refs[units : 2 * units]
    before, out, l, g, ls, gs, stats = refs[2 * units :]
    line, xi = where_am_i()
    advance(ds, dt, own, other, before, known, stats, l, g, ls, gs)

    places = {}
    at = 0
    for steps, partner in ORDER:
        for step in steps:
            places[step, partner] = at
            at += 2 * SHARD
    for step in range(8):
        mine, across = (stats[:4, places[step, p] : places[step, p] + 2 * SHARD] for p in (0, 1))
        v = jnp.concatenate([jnp.where(xi == 0, mine, across), jnp.where(xi == 0, across, mine)], axis=1)
        row = pl.ds(lax.rem(line + step, 8), 1)
        for n in range(4):
            out[0, n, row, :] = v[n : n + 1, :128]
            out[0, 4 + n // 2, row, (n % 2) * 64 : (n % 2 + 1) * 64] = v[n : n + 1, 128:]
    for k in range(1, out.shape[0]):
        out[k] = out[0]


def late(own, other, before, known, ds, dt):
    rows = total_rows(own)
    chunks, done = rows // CHUNK, known // CHUNK
    vmem = pl.BlockSpec(memory_space=pltpu.VMEM)
    work = rows * rows - known * done * CHUNK
    return pl.pallas_call(
        functools.partial(late_kernel, ds, dt, len(own), known),
        out_shape=jax.ShapeDtypeStruct((16, 6, 8, 128), jnp.float32),
        in_specs=[vmem] * (len(own) + len(other) + 1),
        out_specs=vmem,
        scratch_shapes=scratch(rows, known) + [pltpu.VMEM((8, rows), jnp.float32)],
        compiler_params=pltpu.CompilerParams(vmem_limit_bytes=20 * 1024 * 1024),
        cost_estimate=pl.CostEstimate(
            flops=2 * work * (ds + dt), bytes_accessed=8 * rows * (ds + dt), transcendentals=2 * work
        ),
    )(*own, *other, before)


def losses(parts, count, lse, mark, mean, diagonal):
    top, high = lse(0), mark(0)
    for k in range(1, count):
        top = jnp.maximum(top, lse(k))
        high = jnp.maximum(high, mark(k))
    spread = mass = weighted = own = jnp.zeros_like(top)
    for k in range(count):
        e = jnp.exp(mark(k) - high)
        spread += jnp.exp(lse(k) - top)
        mass += e
        weighted += e * mean(k)
        own += diagonal(k)
    return top + jnp.log(spread) - 0.5 * own - 0.5 * weighted / mass


def halves(parts, rows):
    count = parts.shape[0]
    return (
        losses(parts, count, *(lambda k, n=n: parts[k, n, rows, :] for n in range(4))),
        losses(
            parts,
            count,
            *(lambda k, n=n: parts[k, 4 + n // 2, rows, (n % 2) * 64 : (n % 2 + 1) * 64] for n in range(4)),
        ),
    )


def finish_kernel(parts, mine, total, held):
    line, xi = where_am_i()
    one, two = halves(parts, slice(0, 8))
    held[:, :128] = one
    held[:, 128:] = jnp.concatenate([two, two], axis=1)
    v = held[pl.ds(line, 1), :]
    mine[...] = jnp.where(xi == 0, v[:, :128], v[:, 2 * SHARD : 2 * SHARD + 128])
    total[...] = jnp.full(total.shape, jnp.sum(one) + jnp.sum(two), jnp.float32)


def finish(parts):
    vmem = pl.BlockSpec(memory_space=pltpu.VMEM)
    return pl.pallas_call(
        finish_kernel,
        out_shape=(
            jax.ShapeDtypeStruct((1, 128), jnp.float32),
            jax.ShapeDtypeStruct((32, 1, 128), jnp.float32),
        ),
        in_specs=[vmem],
        out_specs=[vmem] * 2,
        scratch_shapes=[pltpu.VMEM((8, 256), jnp.float32)],
        compiler_params=pltpu.CompilerParams(vmem_limit_bytes=4 * 1024 * 1024),
    )(parts)


def shards(image_student, text_student, image_teacher, text_teacher):
    ds, dt = image_student.shape[1], image_teacher.shape[1]
    core = lax.axis_index("img") % 2

    def swap(v):
        return lax.ppermute(v, AXES, CORE_PAIRS)

    mine, theirs = pack(image_student, text_student, image_teacher, text_teacher)
    def pass_on(v):
        return lax.ppermute(v, AXES, X_PAIRS)

    def joined(*v):
        return jnp.concatenate(v, axis=0)

    def after(v, *others):
        return lax.optimization_barrier((v, others))[0]

    chip = joined(mine, swap(theirs))
    up, down = [chip], [chip]
    for _ in range(3):
        up.append(lax.ppermute(up[-1], AXES, UP))
        down.append(lax.ppermute(down[-1], AXES, DOWN))
    near = joined(chip, up[1], down[1])
    near_across = pass_on(near)
    middle = joined(up[2], down[2])
    middle_across = pass_on(middle)
    last = lax.ppermute(up[3], AXES, UP)
    end = after(joined(up[3], down[3], last), near_across, middle_across)
    end_across = pass_on(end)
    own = [near, near_across, middle, middle_across]
    known = total_rows(own)
    other = [swap(v) for v in own]
    before = early(own, other, ds, dt)
    end_other = swap(end)
    across_other = swap(after(end_across, before))
    own.append(end)
    other.append(end_other)
    before = between(own, other, before, known, ds, dt)
    known = total_rows(own)
    stats = late(own + [end_across], other + [across_other], before, known, ds, dt)
    parts = lax.all_to_all(stats, AXES, 0, 0, axis_index_groups=STAT_GROUPS)
    chip, total = finish(parts)
    first, second = chip[0, :SHARD], swap(chip)[0, SHARD : 2 * SHARD]
    image_loss = jnp.where(core == 0, first, second)
    text_loss = jnp.where(core == 0, second, first)
    totals = lax.all_to_all(total, AXES, 0, 0, axis_index_groups=SUM_GROUPS)
    return image_loss, text_loss, jnp.sum(totals[:, 0, 0]) / (2.0 * SHARD * 512)


def solution(mesh):
    spec = P(("img", "txt"), None)
    return jax.shard_map(
        shards,
        mesh=mesh,
        in_specs=(spec, spec, spec, spec),
        out_specs=(P(("img", "txt")), P(("img", "txt")), P()),
        check_vma=False,
    )
```

```python
import functools
import math

import jax
import jax.numpy as jnp
from jax import lax
from jax.experimental import pallas as pl
from jax.experimental.pallas import tpu as pltpu
from jax.sharding import PartitionSpec as P

AXES = ("img", "txt")
LOG2E = 1.0 / math.log(2.0)
LOW = -1e30
SHARD = 48
CHUNK = 256
BLOCK = 128
ORDER = (((0, 7, 1), 0), ((0, 7, 1), 1), ((6, 2), 0), ((6, 2), 1), ((5, 3, 4), 0), ((5, 3, 4), 1))


def place(x, y, z, c):
    return (((x // 2) * 8 + y) * 2 + c) * 16 + z * 2 + x % 2


def everywhere():
    return [
        (x, y, z, c) for x in range(4) for y in range(8) for z in range(8) for c in range(2)
    ]


ROW_X = ((0, 1), (3, 2))
COL_X = ((0, 3), (1, 2))
CORE_PAIRS = [(place(x, y, z, c), place(x, y, z, 1 - c)) for x, y, z, c in everywhere()]
X_PAIRS = [
    (place(x, y, z, c), place(x ^ 1 if c == 0 else 3 - x, y, z, c)) for x, y, z, c in everywhere()
]
UP, DOWN = (
    [
        (place(x, y, z, c), place(x, y, (z + s) % 8, c) if c == 0 else place(x, (y + s) % 8, z, c))
        for x, y, z, c in everywhere()
    ]
    for s in (1, -1)
)
STAT_GROUPS = [[place(x, y, z, 0) for z in range(8) for x in pair] for pair in ROW_X for y in range(8)] + [
    [place(x, y, z, 1) for y in range(8) for x in pair] for pair in COL_X for z in range(8)
]
SUM_GROUPS = [
    [place(pair[e], y, k, 0) for y in range(8) for pair in ROW_X]
    + [place(pair[e], k, z, 1) for z in range(8) for pair in COL_X]
    for k in range(8)
    for e in range(2)
]


def where_am_i():
    img = lax.axis_index("img")
    txt = lax.axis_index("txt")
    x_hi, x_lo = img // 16, txt % 2
    core = img % 2
    return jnp.where(core == 0, txt // 2, (img // 2) % 8), jnp.where(core == 0, x_hi ^ x_lo, x_hi)


def dot(left, right):
    return lax.dot_general(
        left, right, (((1,), (1,)), ((), ())), preferred_element_type=jnp.float32
    )


def pack_kernel(image_s, text_s, image_t, text_t, mine, theirs, sems):
    ds, dt = image_s.shape[1], image_t.shape[1]
    core = lax.axis_index("img") % 2

    def copies(image_out, text_out):
        parts = (pl.ds(0, ds), pl.ds(ds, dt), pl.ds(ds + dt, dt))
        out = []
        for n, source in enumerate((image_s, image_t, text_t)):
            out.append(pltpu.make_async_copy(source, image_out.at[:, parts[n]], sems.at[n]))
        for n, source in enumerate((text_s, text_t, image_t)):
            out.append(pltpu.make_async_copy(source, text_out.at[:, parts[n]], sems.at[3 + n]))
        return out

    @pl.when(core == 0)
    def _():
        for copy in copies(mine, theirs):
            copy.start()

    @pl.when(core == 1)
    def _():
        for copy in copies(theirs, mine):
            copy.start()

    for copy in copies(mine, theirs):
        copy.wait()


def pack(image_s, text_s, image_t, text_t):
    shape = jax.ShapeDtypeStruct((SHARD, image_s.shape[1] + 2 * image_t.shape[1]), jnp.bfloat16)
    return pl.pallas_call(
        pack_kernel,
        out_shape=(shape, shape),
        in_specs=[pl.BlockSpec(memory_space=pl.ANY)] * 4,
        out_specs=[pl.BlockSpec(memory_space=pltpu.VMEM)] * 2,
        scratch_shapes=[pltpu.SemaphoreType.DMA((6,))],
        compiler_params=pltpu.CompilerParams(vmem_limit_bytes=60 * 1024 * 1024),
    )(image_s, text_s, image_t, text_t)


def total_rows(refs):
    return sum(ref.shape[0] for ref in refs)


def piece(refs, start, stop, low, high):
    parts, at = [], 0
    for ref in refs:
        size = ref.shape[0]
        a, b = max(start - at, 0), min(stop - at, size)
        if a < b:
            parts.append(ref[a:b, low:high])
        at += size
    return jnp.concatenate(parts, axis=0) if len(parts) > 1 else parts[0]


def products(ds, dt, own, other, lanes, rows, l, g):
    l[: rows[1] - rows[0], :] = dot(piece(other, *rows, 0, ds), piece(own, *lanes, 0, ds))
    g[: rows[1] - rows[0], :] = dot(piece(other, *rows, ds + dt, ds + 2 * dt), piece(own, *lanes, ds, ds + dt))


def summary(ds, dt, l, g, rows, first):
    kl = 2.0 / math.sqrt(ds) * LOG2E
    kt = 3.0 / math.sqrt(dt) * LOG2E
    diagonal = jnp.zeros((1, CHUNK), jnp.float32)
    if first:
        s = lax.broadcasted_iota(jnp.int32, (2 * SHARD, CHUNK), 0)
        r = lax.broadcasted_iota(jnp.int32, (2 * SHARD, CHUNK), 1)
        same = (r < 2 * SHARD) & (s == jnp.where(r < SHARD, r + SHARD, r - SHARD))
        g[: 2 * SHARD, :] = jnp.where(same, LOW, g[: 2 * SHARD, :])
        diagonal = jnp.sum(jnp.where(same, l[: 2 * SHARD, :], 0.0), axis=0, keepdims=True)
    blocks = [slice(i, min(i + BLOCK, rows)) for i in range(0, rows, BLOCK)]

    def eights(v):
        return v.reshape(v.shape[0] // 8, 8, CHUNK)

    top = high = jnp.full((8, CHUNK), LOW, jnp.float32)
    for here in blocks:
        top = jnp.maximum(top, jnp.max(eights(l[here, :]), axis=0))
        high = jnp.maximum(high, jnp.max(eights(g[here, :]), axis=0))
    top = jnp.max(top, axis=0, keepdims=True)
    high = jnp.max(high, axis=0, keepdims=True)
    total = mass = weighted = jnp.zeros((8, CHUNK), jnp.float32)
    for here in blocks:
        lv = l[here, :]
        e = jnp.exp2((g[here, :] - high) * kt)
        total += jnp.sum(eights(jnp.exp2((lv - top) * kl)), axis=0)
        mass += jnp.sum(eights(e), axis=0)
        weighted += jnp.sum(eights(e * lv), axis=0)
    total = jnp.sum(total, axis=0, keepdims=True)
    mass = jnp.sum(mass, axis=0, keepdims=True)
    weighted = jnp.sum(weighted, axis=0, keepdims=True)
    return (
        top * (kl / LOG2E) + jnp.log(total),
        high * (kt / LOG2E) + jnp.log(mass),
        weighted / mass * (kl / LOG2E),
        diagonal * (kl / LOG2E),
    )


def early_kernel(ds, dt, units, *refs):
    own, other = refs[:units], refs[units : 2 * units]
    out, l, g = refs[2 * units :]
    rows = total_rows(own)
    chunks = rows // CHUNK

    def multiply(j):
        products(ds, dt, own, other, (j * CHUNK, (j + 1) * CHUNK), (0, rows), l.at[j % 2], g.at[j % 2])

    multiply(0)
    for j in range(chunks):
        if j + 1 < chunks:
            multiply(j + 1)
        for n, v in enumerate(summary(ds, dt, l.at[j % 2], g.at[j % 2], rows, j == 0)):
            out[n : n + 1, j * CHUNK : (j + 1) * CHUNK] = v


def early(own, other, ds, dt):
    rows = total_rows(own)
    chunks = rows // CHUNK
    vmem = pl.BlockSpec(memory_space=pltpu.VMEM)
    work = rows * chunks * CHUNK
    return pl.pallas_call(
        functools.partial(early_kernel, ds, dt, len(own)),
        out_shape=jax.ShapeDtypeStruct((8, chunks * CHUNK), jnp.float32),
        in_specs=[vmem] * (len(own) + len(other)),
        out_specs=vmem,
        scratch_shapes=[pltpu.VMEM((2, rows, CHUNK), jnp.float32)] * 2,
        compiler_params=pltpu.CompilerParams(vmem_limit_bytes=20 * 1024 * 1024),
        cost_estimate=pl.CostEstimate(
            flops=2 * work * (ds + dt), bytes_accessed=8 * rows * (ds + dt), transcendentals=2 * work
        ),
    )(*own, *other)


def advance(ds, dt, own, other, before, known, stats, l, g, ls, gs):
    rows = total_rows(own)
    chunks = rows // CHUNK
    done = known // CHUNK

    def lanes(j):
        return j * CHUNK, (j + 1) * CHUNK

    for j in range(done):
        products(ds, dt, own, other, lanes(j), (known, rows), ls.at[j], gs.at[j])
    for j in range(done, chunks):
        products(ds, dt, own, other, lanes(j), (0, rows), l.at[j % 2], g.at[j % 2])
        if j == done:
            for i in range(done):
                to = slice(*lanes(i))
                lse, mark, mean, _ = summary(ds, dt, ls.at[i], gs.at[i], rows - known, False)
                old_lse, old_mark, old_mean = (before[n : n + 1, to] for n in range(3))
                top = jnp.maximum(lse, old_lse)
                stats[0:1, to] = top + jnp.log(jnp.exp(lse - top) + jnp.exp(old_lse - top))
                top = jnp.maximum(mark, old_mark)
                one, two = jnp.exp(mark - top), jnp.exp(old_mark - top)
                stats[1:2, to] = top + jnp.log(one + two)
                stats[2:3, to] = (one * mean + two * old_mean) / (one + two)
                stats[3:4, to] = before[3:4, to]
        else:
            for n, v in enumerate(summary(ds, dt, l.at[(j - 1) % 2], g.at[(j - 1) % 2], rows, False)):
                stats[n : n + 1, slice(*lanes(j - 1))] = v
    for n, v in enumerate(summary(ds, dt, l.at[(chunks - 1) % 2], g.at[(chunks - 1) % 2], rows, False)):
        stats[n : n + 1, slice(*lanes(chunks - 1))] = v


def scratch(rows, known):
    return [pltpu.VMEM((2, rows, CHUNK), jnp.float32)] * 2 + [
        pltpu.VMEM((known // CHUNK, rows - known, CHUNK), jnp.float32)
    ] * 2


def between_kernel(ds, dt, units, known, *refs):
    own, other = refs[:units], refs[units : 2 * units]
    before, out, *work = refs[2 * units :]
    advance(ds, dt, own, other, before, known, out, *work)


def between(own, other, before, known, ds, dt):
    rows = total_rows(own)
    lanes = rows // CHUNK * CHUNK
    vmem = pl.BlockSpec(memory_space=pltpu.VMEM)
    work = rows * lanes - known * before.shape[1]
    return pl.pallas_call(
        functools.partial(between_kernel, ds, dt, len(own), known),
        out_shape=jax.ShapeDtypeStruct((8, lanes), jnp.float32),
        in_specs=[vmem] * (len(own) + len(other) + 1),
        out_specs=vmem,
        scratch_shapes=scratch(rows, known),
        compiler_params=pltpu.CompilerParams(vmem_limit_bytes=20 * 1024 * 1024),
        cost_estimate=pl.CostEstimate(
            flops=2 * work * (ds + dt), bytes_accessed=8 * rows * (ds + dt), transcendentals=2 * work
        ),
    )(*own, *other, before)


def late_kernel(ds, dt, units, known, *refs):
    own, other = refs[:units], refs[units : 2 * units]
    before, out, l, g, ls, gs, stats = refs[2 * units :]
    line, xi = where_am_i()
    advance(ds, dt, own, other, before, known, stats, l, g, ls, gs)

    places = {}
    at = 0
    for steps, partner in ORDER:
        for step in steps:
            places[step, partner] = at
            at += 2 * SHARD
    for step in range(8):
        mine, across = (stats[:4, places[step, p] : places[step, p] + 2 * SHARD] for p in (0, 1))
        v = jnp.concatenate([jnp.where(xi == 0, mine, across), jnp.where(xi == 0, across, mine)], axis=1)
        row = pl.ds(lax.rem(line + step, 8), 1)
        for n in range(3):
            out[0, n, row, :] = v[n : n + 1, :128]
            out[0, 3 + n // 2, row, (n % 2) * 64 : (n % 2 + 1) * 64] = v[n : n + 1, 128:]
        out[0, 4, row, 64:] = v[3:4, :64] + v[3:4, 64:128] + v[3:4, 128:]
    for k in range(1, out.shape[0]):
        out[k] = out[0]


def late(own, other, before, known, ds, dt):
    rows = total_rows(own)
    chunks, done = rows // CHUNK, known // CHUNK
    vmem = pl.BlockSpec(memory_space=pltpu.VMEM)
    work = rows * rows - known * done * CHUNK
    return pl.pallas_call(
        functools.partial(late_kernel, ds, dt, len(own), known),
        out_shape=jax.ShapeDtypeStruct((16, 5, 8, 128), jnp.float32),
        in_specs=[vmem] * (len(own) + len(other) + 1),
        out_specs=vmem,
        scratch_shapes=scratch(rows, known) + [pltpu.VMEM((8, rows), jnp.float32)],
        compiler_params=pltpu.CompilerParams(vmem_limit_bytes=20 * 1024 * 1024),
        cost_estimate=pl.CostEstimate(
            flops=2 * work * (ds + dt), bytes_accessed=8 * rows * (ds + dt), transcendentals=2 * work
        ),
    )(*own, *other, before)


def losses(count, lse, mark, mean):
    top, high = lse(0), mark(0)
    for k in range(1, count):
        top = jnp.maximum(top, lse(k))
        high = jnp.maximum(high, mark(k))
    spread = mass = weighted = jnp.zeros_like(top)
    for k in range(count):
        e = jnp.exp(mark(k) - high)
        spread += jnp.exp(lse(k) - top)
        mass += e
        weighted += e * mean(k)
    return top + jnp.log(spread) - 0.5 * weighted / mass


def halves(parts, rows):
    count = parts.shape[0]
    return (
        losses(count, *(lambda k, n=n: parts[k, n, rows, :] for n in range(3))),
        losses(
            count, *(lambda k, n=n: parts[k, 3 + n // 2, rows, (n % 2) * 64 : (n % 2 + 1) * 64] for n in range(3))
        ),
    )


def finish_kernel(parts, mine, total, held):
    line, xi = where_am_i()
    one, two = halves(parts, slice(0, 8))
    diagonal = jnp.sum(sum(parts[k, 4, :, 64:] for k in range(parts.shape[0])))
    held[:, :128] = one
    held[:, 128:] = jnp.concatenate([two, two], axis=1)
    v = held[pl.ds(line, 1), :]
    mine[...] = jnp.where(xi == 0, v[:, :128], v[:, 2 * SHARD : 2 * SHARD + 128])
    total[...] = jnp.full(total.shape, jnp.sum(one) + jnp.sum(two) - 0.5 * diagonal, jnp.float32)


def finish(parts):
    vmem = pl.BlockSpec(memory_space=pltpu.VMEM)
    return pl.pallas_call(
        finish_kernel,
        out_shape=(
            jax.ShapeDtypeStruct((1, 128), jnp.float32),
            jax.ShapeDtypeStruct((32, 1, 128), jnp.float32),
        ),
        in_specs=[vmem],
        out_specs=[vmem] * 2,
        scratch_shapes=[pltpu.VMEM((8, 256), jnp.float32)],
        compiler_params=pltpu.CompilerParams(vmem_limit_bytes=4 * 1024 * 1024),
    )(parts)


def shards(image_student, text_student, image_teacher, text_teacher):
    ds, dt = image_student.shape[1], image_teacher.shape[1]
    core = lax.axis_index("img") % 2

    def swap(v):
        return lax.ppermute(v, AXES, CORE_PAIRS)

    mine, theirs = pack(image_student, text_student, image_teacher, text_teacher)
    def pass_on(v):
        return lax.ppermute(v, AXES, X_PAIRS)

    def joined(*v):
        return jnp.concatenate(v, axis=0)

    def after(v, *others):
        return lax.optimization_barrier((v, others))[0]

    chip = joined(mine, swap(theirs))
    up, down = [chip], [chip]
    for _ in range(3):
        up.append(lax.ppermute(up[-1], AXES, UP))
        down.append(lax.ppermute(down[-1], AXES, DOWN))
    near = joined(chip, up[1], down[1])
    near_across = pass_on(near)
    middle = joined(up[2], down[2])
    middle_across = pass_on(middle)
    last = lax.ppermute(up[3], AXES, UP)
    end = after(joined(up[3], down[3], last), near_across, middle_across)
    end_across = pass_on(end)
    own = [near, near_across, middle, middle_across]
    known = total_rows(own)
    other = [swap(v) for v in own]
    before = early(own, other, ds, dt)
    end_other = swap(end)
    across_other = swap(after(end_across, before))
    own.append(end)
    other.append(end_other)
    before = between(own, other, before, known, ds, dt)
    known = total_rows(own)
    stats = late(own + [end_across], other + [across_other], before, known, ds, dt)
    parts = lax.all_to_all(stats, AXES, 0, 0, axis_index_groups=STAT_GROUPS)
    chip, total = finish(parts)
    first, second = chip[0, :SHARD], swap(chip)[0, SHARD : 2 * SHARD]
    diagonal = jnp.sum(image_student.astype(jnp.float32) * text_student.astype(jnp.float32), axis=1)
    diagonal *= 1.0 / math.sqrt(ds)
    image_loss = jnp.where(core == 0, first, second) - diagonal
    text_loss = jnp.where(core == 0, second, first) - diagonal
    totals = lax.all_to_all(total, AXES, 0, 0, axis_index_groups=SUM_GROUPS)
    return image_loss, text_loss, jnp.sum(totals[:, 0, 0]) / (2.0 * SHARD * 512)


def solution(mesh):
    spec = P(("img", "txt"), None)
    return jax.shard_map(
        shards,
        mesh=mesh,
        in_specs=(spec, spec, spec, spec),
        out_specs=(P(("img", "txt")), P(("img", "txt")), P()),
        check_vma=False,
    )
```
